32 devices in a mesh: seq: 8 (over z, x), tp: 4 (over y, core).
Axes of the slice: x: 2, y: 2, z: 4, core: 2. Of those that a mesh axis runs over, the one named last changes fastest.
Arguments:
- grad_out: bfloat16 [2048, 4096], P('seq', 'tp'), may hold values from -6 to 6
- out_weight: bfloat16 [4096, 4096], P('tp'), may hold values from -0.09375 to 0.09375
- queries: bfloat16 [2048, 4096], P('seq', 'tp'), may hold values from -45 to 45
- keys: bfloat16 [2048, 4096], P('seq', 'tp'), may hold values from -4 to 4
- values: bfloat16 [2048, 4096], P('seq', 'tp'), may hold values from -6 to 6
- visible: int32 [16, 3], replicated, may hold values from 0 to 15, as said below
- live: int32 [16], replicated, may hold values from 1 to 3
Outputs:
- grad_queries: bfloat16 [2048, 4096], P('seq', 'tp')
- grad_keys: bfloat16 [2048, 4096], P('seq', 'tp')
- grad_values: bfloat16 [2048, 4096], P('seq', 'tp')
The draws below stay inside these ranges and needn't reach their ends.
Inputs may be any that keep to these rules, and one draw needn't show every extreme that they name: `visible`: row a lists blocks that lie on other shards than a's (block b lies on shard b // 2); the rows of one shard never list a block twice, and list at most 1 block of any one other shard, a bound that some shard reaches.
All inputs are finite; a program needn't handle non-finite values.
Results may differ from the reference program's by a relative error of at most 0.014.
Values may be sent and summed in bfloat16 or wider, within the bound.
No kernel may reach another device: no remote copies, remote signals or barrier semaphores. Data moves between devices by JAX's collectives and lax.ppermute only.
A program may use at most 128 MiB of HBM per device.

```python
import math
import jax
import jax.numpy as jnp
from jax import lax

D = 4096
HEADS = 32
D_HEAD = 128
BLK = 128
BLK_DEV = 2
NREM = 3
NBLK = 16
TOKENS = 2048


def paired_rows(key, part):
    array_shape = (TOKENS, HEADS * D_HEAD)
    keys_drawn = jnp.clip(jax.random.normal(jax.random.fold_in(key, 71), array_shape, jnp.float32), -4.0, 4.0)
    queries_drawn = jnp.clip(jax.random.normal(jax.random.fold_in(key, 72), array_shape, jnp.float32), -4.0, 4.0)
    return (queries_drawn, keys_drawn)


def draw_queries(key, part):
    return paired_rows(key, part)[0].astype(jnp.bfloat16)


def draw_keys(key, part):
    return paired_rows(key, part)[1].astype(jnp.bfloat16)


def draw_visible(key, part):
    shard_count = NBLK // BLK_DEV
    others = shard_count - 1
    entries = BLK_DEV * NREM

    def one_shard(shard):
        shard_key = jax.random.fold_in(key, shard)
        ordering = jax.random.permutation(jax.random.fold_in(shard_key, 81), others)
        offsets = jax.random.randint(jax.random.fold_in(shard_key, 82), (shard_count,), 0, BLK_DEV)
        entry = jnp.arange(entries)
        owner = (shard + 1 + ordering[entry % others]) % shard_count
        within = (offsets[owner] + entry // others) % BLK_DEV
        return owner * BLK_DEV + within
    listed = jax.vmap(one_shard)(jnp.arange(shard_count))
    return listed.reshape(NBLK, NREM).astype(jnp.int32)


def draw_live(key, part):
    drawn = jax.random.randint(jax.random.fold_in(key, 91), (NBLK,), 1, NREM + 1)
    return jnp.where(jnp.arange(NBLK) < BLK_DEV, NREM, drawn).astype(jnp.int32)


def block_levels(key, shape, split, smallest, largest):
    def one(dim, blocks):
        draws = jax.random.uniform(jax.random.fold_in(jax.random.fold_in(key, 6), dim), (blocks,), jnp.float32, smallest / len(split), largest / len(split))
        return jnp.repeat(jnp.exp(draws), shape[dim] // blocks).reshape((-1,) + (1,) * (len(shape) - dim - 1))

    loudness = one(*split[0])
    for cut in split[1:]:
        loudness = loudness * one(*cut)
    return loudness


def gaussian(key, dims, width, reach, pieces=(), kind=jnp.bfloat16):
    loudness = block_levels(key, dims, pieces, -0.22, 0.18) if pieces else 1.0
    array = jax.random.normal(key, dims, jnp.float32) * width * loudness
    return jnp.minimum(jnp.maximum(array, -reach), reach).astype(kind)


def setup_inputs(seed: int = 0) -> dict:
    seeds = jax.random.split(jax.random.key(seed), 8)
    return {
        "grad_out": gaussian(seeds[0], (TOKENS, D), 1.0, 6.0, ((0, 8), (1, 4))),
        "out_weight": gaussian(seeds[1], (HEADS * D_HEAD, D), D ** -0.5, 0.09375, ((0, 4),)),
        "queries": draw_queries(jax.random.fold_in(seeds[7], 71), 0),
        "keys": draw_keys(jax.random.fold_in(seeds[7], 71), 0),
        "values": gaussian(seeds[4], (TOKENS, HEADS * D_HEAD), 1.0, 6.0, ((0, 8), (1, 4))),
        "visible": draw_visible(jax.random.fold_in(seeds[7], 71), 0),
        "live": draw_live(jax.random.fold_in(seeds[7], 71), 0),
    }


def rounded(array_in):
    return lax.optimization_barrier(array_in.astype(jnp.bfloat16)).astype(jnp.float32)

def reference(grad_out, out_weight, queries, keys, values, visible, live):
    head_count = HEADS
    feature_width = HEADS * D_HEAD
    row_count = BLK_DEV * BLK
    shard_count = NBLK // BLK_DEV
    scaling = 1.0 / math.sqrt(D_HEAD)
    key_blocks = keys.reshape(NBLK, BLK, feature_width)
    value_blocks = values.reshape(NBLK, BLK, feature_width)

    def one_shard(carry, shard):
        grad_key_acc, grad_value_acc = carry
        first_row = (shard * row_count).astype(jnp.int32)
        first_block = (shard * BLK_DEV).astype(jnp.int32)
        upstream = lax.dynamic_slice_in_dim(grad_out, first_row, row_count, 0)
        dout = jnp.dot(upstream, out_weight.T, preferred_element_type=jnp.float32).astype(jnp.bfloat16)
        dout_rows = dout.astype(jnp.float32).reshape(BLK_DEV, BLK, head_count, D_HEAD)
        query_rows = lax.dynamic_slice_in_dim(queries, first_row, row_count, 0).astype(jnp.float32).reshape(BLK_DEV, BLK, head_count, D_HEAD)
        key_near = lax.dynamic_slice_in_dim(keys, first_row, row_count, 0).astype(jnp.float32).reshape(row_count, head_count, D_HEAD)
        value_near = lax.dynamic_slice_in_dim(values, first_row, row_count, 0).astype(jnp.float32).reshape(row_count, head_count, D_HEAD)
        listed = lax.dynamic_slice_in_dim(visible, first_block, BLK_DEV, 0).reshape(BLK_DEV * NREM).astype(jnp.int32)
        counts = lax.dynamic_slice_in_dim(live, first_block, BLK_DEV, 0)
        key_far = jnp.take(key_blocks, listed, axis=0).astype(jnp.float32).reshape(BLK_DEV, NREM * BLK, head_count, D_HEAD)
        value_far = jnp.take(value_blocks, listed, axis=0).astype(jnp.float32).reshape(BLK_DEV, NREM * BLK, head_count, D_HEAD)
        seen_mask = jnp.repeat(jnp.arange(NREM, dtype=jnp.int32)[None, :] < counts[:, None], BLK, axis=1)
        near_scores = jnp.einsum('aihd,jhd->ahij', query_rows, key_near) * scaling
        far_scores = jnp.einsum('aihd,ajhd->ahij', query_rows, key_far) * scaling
        far_scores = jnp.where(seen_mask[:, None, None, :], far_scores, -1e+30)
        highest = jnp.maximum(lax.optimization_barrier(jnp.max(near_scores, axis=3)), lax.optimization_barrier(jnp.max(far_scores, axis=3)))[..., None]
        near_exp = jnp.exp(near_scores - highest)
        far_exp = jnp.exp(far_scores - highest)
        totals = lax.optimization_barrier(jnp.sum(near_exp, axis=3, keepdims=True)) + lax.optimization_barrier(jnp.sum(far_exp, axis=3, keepdims=True))
        near_probs = near_exp / totals
        far_probs = far_exp / totals
        near_grad = jnp.einsum('aihd,jhd->ahij', dout_rows, value_near)
        far_grad = jnp.einsum('aihd,ajhd->ahij', dout_rows, value_far)
        row_delta = lax.optimization_barrier(jnp.sum(near_probs * near_grad, axis=3, keepdims=True)) + lax.optimization_barrier(jnp.sum(far_probs * far_grad, axis=3, keepdims=True))
        near_ds = rounded(near_probs * (near_grad - row_delta) * scaling)
        far_ds = rounded(far_probs * (far_grad - row_delta) * scaling)
        grad_query = jnp.einsum('ahij,jhd->aihd', near_ds, key_near) + jnp.einsum('ahij,ajhd->aihd', far_ds, key_far)
        grad_query = grad_query.reshape(row_count, feature_width).astype(jnp.bfloat16)
        near_key_term = jnp.einsum('ahij,aihd->jhd', near_ds, query_rows).reshape(BLK_DEV, BLK, feature_width)
        near_value_term = jnp.einsum('ahij,aihd->jhd', rounded(near_probs), dout_rows).reshape(BLK_DEV, BLK, feature_width)
        far_key_term = rounded(jnp.einsum('ahij,aihd->ajhd', far_ds, query_rows)).reshape(BLK_DEV * NREM, BLK, feature_width)
        far_value_term = rounded(jnp.einsum('ahij,aihd->ajhd', rounded(far_probs), dout_rows)).reshape(BLK_DEV * NREM, BLK, feature_width)
        grad_key_acc = grad_key_acc.at[listed].add(far_key_term)
        grad_value_acc = grad_value_acc.at[listed].add(far_value_term)
        own_keys = lax.dynamic_slice_in_dim(grad_key_acc, first_block, BLK_DEV, 0) + near_key_term
        own_values = lax.dynamic_slice_in_dim(grad_value_acc, first_block, BLK_DEV, 0) + near_value_term
        grad_key_acc = lax.dynamic_update_slice_in_dim(grad_key_acc, own_keys, first_block, 0)
        grad_value_acc = lax.dynamic_update_slice_in_dim(grad_value_acc, own_values, first_block, 0)
        return ((grad_key_acc, grad_value_acc), grad_query)
    start = (jnp.zeros((NBLK, BLK, feature_width), jnp.float32), jnp.zeros((NBLK, BLK, feature_width), jnp.float32))
    (grad_key_acc, grad_value_acc), grad_query_all = lax.scan(one_shard, start, jnp.arange(shard_count, dtype=jnp.int32))
    grad_queries = grad_query_all.reshape(TOKENS, feature_width)
    grad_keys = grad_key_acc.reshape(TOKENS, feature_width).astype(jnp.bfloat16)
    grad_values = grad_value_acc.reshape(TOKENS, feature_width).astype(jnp.bfloat16)
    return (grad_queries, grad_keys, grad_values)
```

```python
import functools
import math

import jax
import jax.numpy as jnp
from jax import lax
from jax.experimental import pallas as pl
from jax.experimental.pallas import tpu as pltpu
from jax.sharding import PartitionSpec as P

D_HEAD = 128
BLK = 128
BLK_DEV = 2
NREM = 3


def project_part(out_weight, piece):
    return lax.dot_general(
        piece, out_weight, (((1,), (1,)), ((), ())), preferred_element_type=jnp.float32
    )


def attend_group(query_group, dout_group, key_far, value_far, seen_mask, key_near, value_near):
    scaling = 1.0 / math.sqrt(D_HEAD)
    near_scores = (
        jnp.einsum("aihd,jhd->ahij", query_group, key_near, preferred_element_type=jnp.float32)
        * scaling
    )
    far_scores = (
        jnp.einsum("aihd,ajhd->ahij", query_group, key_far, preferred_element_type=jnp.float32)
        * scaling
    )
    far_scores = jnp.where(seen_mask[:, None, None, :], far_scores, -1e30)
    highest = jnp.maximum(jnp.max(near_scores, axis=3), jnp.max(far_scores, axis=3))[..., None]
    near_exp = jnp.exp(near_scores - highest)
    far_exp = jnp.exp(far_scores - highest)
    totals = jnp.sum(near_exp, axis=3, keepdims=True) + jnp.sum(far_exp, axis=3, keepdims=True)
    near_probs = near_exp / totals
    far_probs = far_exp / totals
    near_grad = jnp.einsum(
        "aihd,jhd->ahij", dout_group, value_near, preferred_element_type=jnp.float32
    )
    far_grad = jnp.einsum(
        "aihd,ajhd->ahij", dout_group, value_far, preferred_element_type=jnp.float32
    )
    row_delta = jnp.sum(near_probs * near_grad, axis=3, keepdims=True) + jnp.sum(
        far_probs * far_grad, axis=3, keepdims=True
    )
    near_ds = (near_probs * (near_grad - row_delta) * scaling).astype(jnp.bfloat16)
    far_ds = (far_probs * (far_grad - row_delta) * scaling).astype(jnp.bfloat16)
    grad_query = jnp.einsum("ahij,jhd->aihd", near_ds, key_near, preferred_element_type=jnp.float32)
    grad_query = grad_query + jnp.einsum(
        "ahij,ajhd->aihd", far_ds, key_far, preferred_element_type=jnp.float32
    )
    log_totals = (highest + jnp.log(totals))[..., 0]
    return (
        near_probs,
        far_probs,
        near_ds,
        far_ds,
        grad_query.astype(jnp.bfloat16),
        log_totals,
        row_delta[..., 0],
    )


def shards_general(grad_out, out_weight, queries, keys, values, visible, live):
    shard_count = lax.axis_size("seq")
    myself = lax.axis_index("seq")
    row_count, feature_width = queries.shape
    head_count = feature_width // D_HEAD
    entries = BLK_DEV * NREM
    capacity = min(BLK_DEV, -(-entries // (shard_count - 1)))
    slot_count = shard_count * capacity
    dout = project_part(out_weight, lax.all_gather(grad_out, "tp", axis=1, tiled=True)).astype(
        jnp.bfloat16
    )
    owners = (visible // BLK_DEV).reshape(shard_count, entries)
    block_within = (visible % BLK_DEV).reshape(shard_count, entries)
    living = (jnp.arange(NREM, dtype=jnp.int32)[None, :] < live[:, None]).reshape(
        shard_count, entries
    )
    positions = jnp.arange(entries, dtype=jnp.int32)
    earlier = positions[None, :] < positions[:, None]
    matching = (owners[:, :, None] == owners[:, None, :]) & living[:, None, :] & earlier[None, :, :]
    ranking = jnp.sum(matching.astype(jnp.int32), axis=2)
    slot_ids = jnp.arange(capacity, dtype=jnp.int32)
    chosen = (living & (owners == myself))[:, None, :] & (
        ranking[:, None, :] == slot_ids[None, :, None]
    )
    filled = jnp.any(chosen, axis=2).reshape(slot_count)
    send_index = jnp.sum(jnp.where(chosen, block_within[:, None, :], 0), axis=2).reshape(slot_count)
    key_blocks = keys.reshape(BLK_DEV, BLK, feature_width)
    value_blocks = values.reshape(BLK_DEV, BLK, feature_width)
    keep_slot = filled[:, None, None]
    send_keys = jnp.where(
        keep_slot, jnp.take(key_blocks, send_index, axis=0), jnp.zeros((), keys.dtype)
    )
    send_values = jnp.where(
        keep_slot, jnp.take(value_blocks, send_index, axis=0), jnp.zeros((), values.dtype)
    )
    fetched_keys, fetched_values = (
        lax.all_to_all(
            send_keys.reshape(shard_count, capacity, BLK, feature_width),
            "seq",
            split_axis=0,
            concat_axis=0,
            tiled=True,
        ),
        lax.all_to_all(
            send_values.reshape(shard_count, capacity, BLK, feature_width),
            "seq",
            split_axis=0,
            concat_axis=0,
            tiled=True,
        ),
    )
    my_owners = lax.dynamic_index_in_dim(owners, myself, 0, keepdims=False)
    my_ranks = lax.dynamic_index_in_dim(ranking, myself, 0, keepdims=False)
    my_living = lax.dynamic_index_in_dim(living, myself, 0, keepdims=False)
    fetch_index = my_owners * capacity + my_ranks
    key_far = jnp.take(fetched_keys.reshape(slot_count, BLK, feature_width), fetch_index, axis=0)
    value_far = jnp.take(
        fetched_values.reshape(slot_count, BLK, feature_width), fetch_index, axis=0
    )
    placement = (
        (jnp.arange(slot_count, dtype=jnp.int32)[:, None] == fetch_index[None, :])
        & my_living[None, :]
    ).astype(jnp.bfloat16)
    collect = (
        (jnp.arange(BLK_DEV, dtype=jnp.int32)[:, None] == send_index[None, :]) & filled[None, :]
    ).astype(jnp.bfloat16)
    group_size = math.gcd(BLK_DEV, max(1, 512 // BLK))
    group_count = BLK_DEV // group_size

    def grouped(array_in):
        return array_in.reshape((group_count, group_size) + array_in.shape[1:])

    query_blocks = grouped(queries.reshape(BLK_DEV, BLK, head_count, D_HEAD))
    dout_blocks = grouped(dout.reshape(BLK_DEV, BLK, head_count, D_HEAD))
    far_key_blocks = grouped(key_far.reshape(BLK_DEV, NREM * BLK, head_count, D_HEAD))
    far_value_blocks = grouped(value_far.reshape(BLK_DEV, NREM * BLK, head_count, D_HEAD))
    seen_blocks = grouped(jnp.repeat(my_living.reshape(BLK_DEV, NREM), BLK, axis=1))
    key_near = keys.reshape(row_count, head_count, D_HEAD)
    value_near = values.reshape(row_count, head_count, D_HEAD)

    def one_group(carry, inputs):
        near_key_acc, near_value_acc = carry
        query_group, dout_group, key_group, value_group, mask_group = inputs
        near_probs, far_probs, near_ds, far_ds, grad_query, log_totals, row_delta = attend_group(
            query_group, dout_group, key_group, value_group, mask_group, key_near, value_near
        )
        near_key_acc = near_key_acc + jnp.einsum(
            "ahij,aihd->jhd", near_ds, query_group, preferred_element_type=jnp.float32
        )
        near_value_acc = near_value_acc + jnp.einsum(
            "ahij,aihd->jhd",
            near_probs.astype(jnp.bfloat16),
            dout_group,
            preferred_element_type=jnp.float32,
        )
        far_key_term = jnp.einsum(
            "ahij,aihd->ajhd", far_ds, query_group, preferred_element_type=jnp.float32
        ).astype(jnp.bfloat16)
        far_value_term = jnp.einsum(
            "ahij,aihd->ajhd",
            far_probs.astype(jnp.bfloat16),
            dout_group,
            preferred_element_type=jnp.float32,
        ).astype(jnp.bfloat16)
        extra = (far_key_term, far_value_term)
        return ((near_key_acc, near_value_acc), (grad_query, extra))

    start = (
        jnp.zeros((row_count, head_count, D_HEAD), jnp.float32),
        jnp.zeros((row_count, head_count, D_HEAD), jnp.float32),
    )
    (near_keys, near_values), (grad_query_all, extra_all) = lax.scan(
        one_group, start, (query_blocks, dout_blocks, far_key_blocks, far_value_blocks, seen_blocks)
    )
    grad_queries = grad_query_all.reshape(row_count, feature_width)
    far_key_terms = extra_all[0].reshape(entries, BLK * feature_width)
    far_value_terms = extra_all[1].reshape(entries, BLK * feature_width)
    returned_keys = jnp.dot(placement, far_key_terms, preferred_element_type=jnp.float32).astype(
        jnp.bfloat16
    )
    returned_values = jnp.dot(
        placement, far_value_terms, preferred_element_type=jnp.float32
    ).astype(jnp.bfloat16)
    back_keys, back_values = (
        lax.all_to_all(
            returned_keys.reshape(shard_count, capacity, BLK, feature_width),
            "seq",
            split_axis=0,
            concat_axis=0,
            tiled=True,
        ),
        lax.all_to_all(
            returned_values.reshape(shard_count, capacity, BLK, feature_width),
            "seq",
            split_axis=0,
            concat_axis=0,
            tiled=True,
        ),
    )
    far_key_sum = jnp.dot(
        collect,
        back_keys.reshape(slot_count, BLK * feature_width),
        preferred_element_type=jnp.float32,
    )
    far_value_sum = jnp.dot(
        collect,
        back_values.reshape(slot_count, BLK * feature_width),
        preferred_element_type=jnp.float32,
    )
    grad_keys = (
        near_keys.reshape(row_count, feature_width) + far_key_sum.reshape(row_count, feature_width)
    ).astype(jnp.bfloat16)
    grad_values = (
        near_values.reshape(row_count, feature_width)
        + far_value_sum.reshape(row_count, feature_width)
    ).astype(jnp.bfloat16)
    return (grad_queries, grad_keys, grad_values)


CUBE = 8
SLOTS = 10
SEEN = (BLK_DEV + NREM) * BLK


def load_seen(me, visible_ref, near_ref, far_refs, slots_ref, seen_ref):
    at = 0
    for ref in far_refs:
        for i in range(ref.shape[0] // BLK):
            slots_ref[at] = ref[i * BLK : (i + 1) * BLK, :]
            at += 1
    for a in range(BLK_DEV):
        seen_ref[a, : BLK_DEV * BLK, :] = near_ref[...]
        for j in range(NREM):
            seen_ref[a, pl.ds((BLK_DEV + j) * BLK, BLK), :] = slots_ref[
                slot_of(me, visible_ref, a, j)
            ]


def slot_of(me, visible_ref, a, j):
    listed = visible_ref[(me * BLK_DEV + a) * NREM + j]
    apart = (listed // BLK_DEV) ^ me
    row = apart // 2
    return jnp.where(apart % 2 == 0, (row - 1) * BLK_DEV + listed % BLK_DEV, 6 + row)


def store_slots(me, visible_ref, terms, slots_ref, out_refs):
    slots_ref[...] = jnp.zeros_like(slots_ref)
    for a in range(BLK_DEV):
        for j in range(NREM):
            slots_ref[slot_of(me, visible_ref, a, j)] = terms[a][
                (BLK_DEV + j) * BLK : (BLK_DEV + j + 1) * BLK, :
            ].astype(jnp.bfloat16)
    at = 0
    for ref in out_refs:
        for i in range(ref.shape[0] // BLK):
            ref[i * BLK : (i + 1) * BLK, :] = slots_ref[at]
            at += 1


def dot_nt(a, b):
    return lax.dot_general(a, b, (((1,), (1,)), ((), ())), preferred_element_type=jnp.float32)


def dot_tn(a, b):
    return lax.dot_general(a, b, (((0,), (0,)), ((), ())), preferred_element_type=jnp.float32)


def probs_of(query, seen, live):
    scores = dot_nt(query, seen) * (1.0 / math.sqrt(D_HEAD))
    column = lax.broadcasted_iota(jnp.int32, scores.shape, 1)
    scores = jnp.where(column < (BLK_DEV + live) * BLK, scores, -1e30)
    raised = jnp.exp(scores - jnp.max(scores, axis=1, keepdims=True))
    return raised / jnp.sum(raised, axis=1, keepdims=True)


def value_kernel(me_ref, visible_ref, live_ref, q, do, k, k1, k2, k3, kxa, kxb, kxc,
                 dv, b1, b2, b3, xa, xb, xc, slots, seen):
    me = me_ref[0]
    load_seen(me, visible_ref, k, (k1, k2, k3, kxa, kxb, kxc), slots, seen)
    terms = []
    for a in range(BLK_DEV):
        rows = slice(a * BLK, (a + 1) * BLK)
        probs = probs_of(q[rows, :], seen[a], live_ref[me * BLK_DEV + a])
        terms.append(dot_tn(probs.astype(jnp.bfloat16), do[rows, :]))
    dv[...] = sum(term[: BLK_DEV * BLK, :] for term in terms)
    store_slots(me, visible_ref, terms, slots, (b1, b2, b3, xa, xb, xc))


def key_kernel(me_ref, visible_ref, live_ref, q, do, k, k1, k2, k3, kxa, kxb, kxc,
               v, v1, v2, v3, vxa, vxb, vxc,
               dq, dk, b1, b2, b3, xa, xb, xc, slots, seen, seen_v):
    me = me_ref[0]
    load_seen(me, visible_ref, k, (k1, k2, k3, kxa, kxb, kxc), slots, seen)
    load_seen(me, visible_ref, v, (v1, v2, v3, vxa, vxb, vxc), slots, seen_v)
    terms = []
    for a in range(BLK_DEV):
        rows = slice(a * BLK, (a + 1) * BLK)
        probs = probs_of(q[rows, :], seen[a], live_ref[me * BLK_DEV + a])
        dprob = dot_nt(do[rows, :], seen_v[a])
        delta = jnp.sum(probs * dprob, axis=1, keepdims=True)
        ds = (probs * (dprob - delta) * (1.0 / math.sqrt(D_HEAD))).astype(jnp.bfloat16)
        dq[rows, :] = jnp.dot(ds, seen[a], preferred_element_type=jnp.float32).astype(jnp.bfloat16)
        terms.append(dot_tn(ds, q[rows, :]))
    dk[...] = sum(term[: BLK_DEV * BLK, :] for term in terms)
    store_slots(me, visible_ref, terms, slots, (b1, b2, b3, xa, xb, xc))


def by_head(kernel, scalars, arrays, outs, scratch, flops):
    def spec(array):
        return pl.BlockSpec((array.shape[0], D_HEAD), lambda h, *_: (0, h))

    width = arrays[0].shape[1]
    out_shape = [jax.ShapeDtypeStruct((rows, width), kind) for rows, kind in outs]
    return pl.pallas_call(
        kernel,
        out_shape=out_shape,
        grid_spec=pltpu.PrefetchScalarGridSpec(
            num_scalar_prefetch=len(scalars),
            grid=(width // D_HEAD,),
            in_specs=[spec(array) for array in arrays],
            out_specs=[spec(array) for array in out_shape],
            scratch_shapes=scratch,
        ),
        compiler_params=pltpu.CompilerParams(vmem_limit_bytes=32 * 1024 * 1024),
        cost_estimate=pl.CostEstimate(
            flops=flops, bytes_accessed=16 * 1024 * 1024, transcendentals=0
        ),
    )(*scalars, *arrays)


def shards_cube(grad_out, out_weight, queries, keys, values, visible, live):
    myself = lax.axis_index("seq")
    row_count, feature_width = queries.shape
    other = myself ^ 1

    def hop(array, distance):
        return lax.ppermute(array, "seq", [(i, i ^ distance) for i in range(CUBE)])

    listed = lax.dynamic_slice_in_dim(visible, other * BLK_DEV, BLK_DEV, 0).reshape(-1)
    apart = (listed // BLK_DEV) ^ other
    wanted = [jnp.sum(jnp.where(apart == 2 * r + 1, listed % BLK_DEV, 0)) for r in range(CUBE // 2)]

    def pick(array, r):
        return lax.dynamic_slice_in_dim(array, wanted[r] * BLK, BLK, 0)

    def place(block, r):
        row = lax.broadcasted_iota(jnp.int32, (row_count, 1), 0) // BLK
        return jnp.where(row == wanted[r], jnp.concatenate([block, block], axis=0), 0)

    def spread(array):
        two = hop(array, 4)
        one = hop(array, 2)
        three = hop(two, 2)
        x_low = hop(jnp.concatenate([pick(array, 0), pick(one, 1)], axis=0), 1)
        x_two = hop(pick(two, 2), 1)
        x_three = hop(pick(three, 3), 1)
        return (one, two, three, x_low, x_two, x_three)

    def gather_sum(near, one, two, three, x_low, x_two, x_three):
        x_three = hop(x_three, 1)
        x_two = hop(x_two, 1)
        x_low = hop(x_low, 1)
        f32 = jnp.float32
        three = hop((three.astype(f32) + place(x_three, 3).astype(f32)).astype(jnp.bfloat16), 2)
        two = hop(
            (two.astype(f32) + place(x_two, 2).astype(f32) + three.astype(f32)).astype(jnp.bfloat16), 4
        )
        one = hop(
            (one.astype(f32) + place(x_low[BLK:], 1).astype(f32)).astype(jnp.bfloat16), 2
        )
        total = near + place(x_low[:BLK], 0).astype(f32) + one.astype(f32) + two.astype(f32)
        return total.astype(jnp.bfloat16)

    far_keys = spread(keys)
    late_values, _ = lax.optimization_barrier((values, far_keys[1]))
    far_values = spread(late_values)
    dout = project_part(out_weight, lax.all_gather(grad_out, "tp", axis=1, tiled=True)).astype(
        jnp.bfloat16
    )
    scalars = (myself.reshape(1), visible.reshape(-1), live)
    f32, bf16 = jnp.float32, jnp.bfloat16
    far_outs = [(2 * BLK, bf16)] * 4 + [(BLK, bf16)] * 2
    slots = pltpu.VMEM((SLOTS, BLK, D_HEAD), bf16)
    seen = pltpu.VMEM((BLK_DEV, SEEN, D_HEAD), bf16)
    product = 2 * row_count * SEEN * feature_width
    dv = by_head(
        value_kernel, scalars, (queries, dout, keys, *far_keys),
        [(row_count, f32)] + far_outs, [slots, seen], 2 * product,
    )
    grad_values = gather_sum(*dv)
    dq, *dk = by_head(
        key_kernel, scalars, (queries, dout, keys, *far_keys, values, *far_values),
        [(row_count, bf16), (row_count, f32)] + far_outs, [slots, seen, seen], 4 * product,
    )
    grad_keys = gather_sum(*dk)
    return (dq, grad_keys, grad_values)


def solution(mesh):
    placed = (
        P("seq", "tp"),
        P("tp", None),
        P("seq", "tp"),
        P("seq", "tp"),
        P("seq", "tp"),
        P(),
        P(),
    )
    return jax.shard_map(
        shards_cube if mesh.shape["seq"] == CUBE else shards_general,
        mesh=mesh,
        in_specs=placed,
        out_specs=(P("seq", "tp"), P("seq", "tp"), P("seq", "tp")),
        check_vma=False,
    )
```

```python
import functools
import math

import jax
import jax.numpy as jnp
from jax import lax
from jax.experimental import pallas as pl
from jax.experimental.pallas import tpu as pltpu
from jax.sharding import PartitionSpec as P

D_HEAD = 128
BLK = 128
BLK_DEV = 2
NREM = 3


def project_part(out_weight, piece):
    return lax.dot_general(
        piece, out_weight, (((1,), (1,)), ((), ())), preferred_element_type=jnp.float32
    )


def attend_group(query_group, dout_group, key_far, value_far, seen_mask, key_near, value_near):
    scaling = 1.0 / math.sqrt(D_HEAD)
    near_scores = (
        jnp.einsum("aihd,jhd->ahij", query_group, key_near, preferred_element_type=jnp.float32)
        * scaling
    )
    far_scores = (
        jnp.einsum("aihd,ajhd->ahij", query_group, key_far, preferred_element_type=jnp.float32)
        * scaling
    )
    far_scores = jnp.where(seen_mask[:, None, None, :], far_scores, -1e30)
    highest = jnp.maximum(jnp.max(near_scores, axis=3), jnp.max(far_scores, axis=3))[..., None]
    near_exp = jnp.exp(near_scores - highest)
    far_exp = jnp.exp(far_scores - highest)
    totals = jnp.sum(near_exp, axis=3, keepdims=True) + jnp.sum(far_exp, axis=3, keepdims=True)
    near_probs = near_exp / totals
    far_probs = far_exp / totals
    near_grad = jnp.einsum(
        "aihd,jhd->ahij", dout_group, value_near, preferred_element_type=jnp.float32
    )
    far_grad = jnp.einsum(
        "aihd,ajhd->ahij", dout_group, value_far, preferred_element_type=jnp.float32
    )
    row_delta = jnp.sum(near_probs * near_grad, axis=3, keepdims=True) + jnp.sum(
        far_probs * far_grad, axis=3, keepdims=True
    )
    near_ds = (near_probs * (near_grad - row_delta) * scaling).astype(jnp.bfloat16)
    far_ds = (far_probs * (far_grad - row_delta) * scaling).astype(jnp.bfloat16)
    grad_query = jnp.einsum("ahij,jhd->aihd", near_ds, key_near, preferred_element_type=jnp.float32)
    grad_query = grad_query + jnp.einsum(
        "ahij,ajhd->aihd", far_ds, key_far, preferred_element_type=jnp.float32
    )
    log_totals = (highest + jnp.log(totals))[..., 0]
    return (
        near_probs,
        far_probs,
        near_ds,
        far_ds,
        grad_query.astype(jnp.bfloat16),
        log_totals,
        row_delta[..., 0],
    )


def shards_general(grad_out, out_weight, queries, keys, values, visible, live):
    shard_count = lax.axis_size("seq")
    myself = lax.axis_index("seq")
    row_count, feature_width = queries.shape
    head_count = feature_width // D_HEAD
    entries = BLK_DEV * NREM
    capacity = min(BLK_DEV, -(-entries // (shard_count - 1)))
    slot_count = shard_count * capacity
    dout = project_part(out_weight, lax.all_gather(grad_out, "tp", axis=1, tiled=True)).astype(
        jnp.bfloat16
    )
    owners = (visible // BLK_DEV).reshape(shard_count, entries)
    block_within = (visible % BLK_DEV).reshape(shard_count, entries)
    living = (jnp.arange(NREM, dtype=jnp.int32)[None, :] < live[:, None]).reshape(
        shard_count, entries
    )
    positions = jnp.arange(entries, dtype=jnp.int32)
    earlier = positions[None, :] < positions[:, None]
    matching = (owners[:, :, None] == owners[:, None, :]) & living[:, None, :] & earlier[None, :, :]
    ranking = jnp.sum(matching.astype(jnp.int32), axis=2)
    slot_ids = jnp.arange(capacity, dtype=jnp.int32)
    chosen = (living & (owners == myself))[:, None, :] & (
        ranking[:, None, :] == slot_ids[None, :, None]
    )
    filled = jnp.any(chosen, axis=2).reshape(slot_count)
    send_index = jnp.sum(jnp.where(chosen, block_within[:, None, :], 0), axis=2).reshape(slot_count)
    key_blocks = keys.reshape(BLK_DEV, BLK, feature_width)
    value_blocks = values.reshape(BLK_DEV, BLK, feature_width)
    keep_slot = filled[:, None, None]
    send_keys = jnp.where(
        keep_slot, jnp.take(key_blocks, send_index, axis=0), jnp.zeros((), keys.dtype)
    )
    send_values = jnp.where(
        keep_slot, jnp.take(value_blocks, send_index, axis=0), jnp.zeros((), values.dtype)
    )
    fetched_keys, fetched_values = (
        lax.all_to_all(
            send_keys.reshape(shard_count, capacity, BLK, feature_width),
            "seq",
            split_axis=0,
            concat_axis=0,
            tiled=True,
        ),
        lax.all_to_all(
            send_values.reshape(shard_count, capacity, BLK, feature_width),
            "seq",
            split_axis=0,
            concat_axis=0,
            tiled=True,
        ),
    )
    my_owners = lax.dynamic_index_in_dim(owners, myself, 0, keepdims=False)
    my_ranks = lax.dynamic_index_in_dim(ranking, myself, 0, keepdims=False)
    my_living = lax.dynamic_index_in_dim(living, myself, 0, keepdims=False)
    fetch_index = my_owners * capacity + my_ranks
    key_far = jnp.take(fetched_keys.reshape(slot_count, BLK, feature_width), fetch_index, axis=0)
    value_far = jnp.take(
        fetched_values.reshape(slot_count, BLK, feature_width), fetch_index, axis=0
    )
    placement = (
        (jnp.arange(slot_count, dtype=jnp.int32)[:, None] == fetch_index[None, :])
        & my_living[None, :]
    ).astype(jnp.bfloat16)
    collect = (
        (jnp.arange(BLK_DEV, dtype=jnp.int32)[:, None] == send_index[None, :]) & filled[None, :]
    ).astype(jnp.bfloat16)
    group_size = math.gcd(BLK_DEV, max(1, 512 // BLK))
    group_count = BLK_DEV // group_size

    def grouped(array_in):
        return array_in.reshape((group_count, group_size) + array_in.shape[1:])

    query_blocks = grouped(queries.reshape(BLK_DEV, BLK, head_count, D_HEAD))
    dout_blocks = grouped(dout.reshape(BLK_DEV, BLK, head_count, D_HEAD))
    far_key_blocks = grouped(key_far.reshape(BLK_DEV, NREM * BLK, head_count, D_HEAD))
    far_value_blocks = grouped(value_far.reshape(BLK_DEV, NREM * BLK, head_count, D_HEAD))
    seen_blocks = grouped(jnp.repeat(my_living.reshape(BLK_DEV, NREM), BLK, axis=1))
    key_near = keys.reshape(row_count, head_count, D_HEAD)
    value_near = values.reshape(row_count, head_count, D_HEAD)

    def one_group(carry, inputs):
        near_key_acc, near_value_acc = carry
        query_group, dout_group, key_group, value_group, mask_group = inputs
        near_probs, far_probs, near_ds, far_ds, grad_query, log_totals, row_delta = attend_group(
            query_group, dout_group, key_group, value_group, mask_group, key_near, value_near
        )
        near_key_acc = near_key_acc + jnp.einsum(
            "ahij,aihd->jhd", near_ds, query_group, preferred_element_type=jnp.float32
        )
        near_value_acc = near_value_acc + jnp.einsum(
            "ahij,aihd->jhd",
            near_probs.astype(jnp.bfloat16),
            dout_group,
            preferred_element_type=jnp.float32,
        )
        far_key_term = jnp.einsum(
            "ahij,aihd->ajhd", far_ds, query_group, preferred_element_type=jnp.float32
        ).astype(jnp.bfloat16)
        far_value_term = jnp.einsum(
            "ahij,aihd->ajhd",
            far_probs.astype(jnp.bfloat16),
            dout_group,
            preferred_element_type=jnp.float32,
        ).astype(jnp.bfloat16)
        extra = (far_key_term, far_value_term)
        return ((near_key_acc, near_value_acc), (grad_query, extra))

    start = (
        jnp.zeros((row_count, head_count, D_HEAD), jnp.float32),
        jnp.zeros((row_count, head_count, D_HEAD), jnp.float32),
    )
    (near_keys, near_values), (grad_query_all, extra_all) = lax.scan(
        one_group, start, (query_blocks, dout_blocks, far_key_blocks, far_value_blocks, seen_blocks)
    )
    grad_queries = grad_query_all.reshape(row_count, feature_width)
    far_key_terms = extra_all[0].reshape(entries, BLK * feature_width)
    far_value_terms = extra_all[1].reshape(entries, BLK * feature_width)
    returned_keys = jnp.dot(placement, far_key_terms, preferred_element_type=jnp.float32).astype(
        jnp.bfloat16
    )
    returned_values = jnp.dot(
        placement, far_value_terms, preferred_element_type=jnp.float32
    ).astype(jnp.bfloat16)
    back_keys, back_values = (
        lax.all_to_all(
            returned_keys.reshape(shard_count, capacity, BLK, feature_width),
            "seq",
            split_axis=0,
            concat_axis=0,
            tiled=True,
        ),
        lax.all_to_all(
            returned_values.reshape(shard_count, capacity, BLK, feature_width),
            "seq",
            split_axis=0,
            concat_axis=0,
            tiled=True,
        ),
    )
    far_key_sum = jnp.dot(
        collect,
        back_keys.reshape(slot_count, BLK * feature_width),
        preferred_element_type=jnp.float32,
    )
    far_value_sum = jnp.dot(
        collect,
        back_values.reshape(slot_count, BLK * feature_width),
        preferred_element_type=jnp.float32,
    )
    grad_keys = (
        near_keys.reshape(row_count, feature_width) + far_key_sum.reshape(row_count, feature_width)
    ).astype(jnp.bfloat16)
    grad_values = (
        near_values.reshape(row_count, feature_width)
        + far_value_sum.reshape(row_count, feature_width)
    ).astype(jnp.bfloat16)
    return (grad_queries, grad_keys, grad_values)


CUBE = 8
SLOTS = 10
SEEN = (BLK_DEV + NREM) * BLK
SMALL = pl.CostEstimate(flops=1, bytes_accessed=1, transcendentals=0)
SCALING = 1.0 / math.sqrt(D_HEAD)


def slot_of(me, visible_ref, a, j):
    listed = visible_ref[(me * BLK_DEV + a) * NREM + j]
    apart = (listed // BLK_DEV) ^ me
    row = apart // 2
    return jnp.where(apart % 2 == 0, (row - 1) * BLK_DEV + listed % BLK_DEV, 6 + row)


def entries_of(me_ref, visible_ref, live_ref):
    me = me_ref[0]
    slots = [[slot_of(me, visible_ref, a, j) for j in range(NREM)] for a in range(BLK_DEV)]
    return slots, [live_ref[me * BLK_DEV + a] for a in range(BLK_DEV)]


def dot(a, b):
    return jnp.dot(a, b, preferred_element_type=jnp.float32)


def dot_nt(a, b):
    return lax.dot_general(a, b, (((1,), (1,)), ((), ())), preferred_element_type=jnp.float32)


def dot_tn(a, b):
    return lax.dot_general(a, b, (((0,), (0,)), ((), ())), preferred_element_type=jnp.float32)


def blocks_of(refs):
    return [(ref, i * BLK) for ref in refs for i in range(ref.shape[0] // BLK)]


def fill(refs, slots_ref):
    def one_head(head, columns):
        for at, (ref, row) in enumerate(blocks_of(refs)):
            slots_ref[at, :, columns] = ref[row : row + BLK, columns]

    over_heads(slots_ref.shape[2] // D_HEAD, 1, one_head)


def clear(slots_ref):
    def one_head(head, columns):
        for at in range(slots_ref.shape[0]):
            slots_ref[at, :, columns] = jnp.zeros((BLK, D_HEAD), slots_ref.dtype)

    over_heads(slots_ref.shape[2] // D_HEAD, 1, one_head)


def drain(slots_ref, refs):
    def one_head(head, columns):
        for at, (ref, row) in enumerate(blocks_of(refs)):
            ref[row : row + BLK, columns] = slots_ref[at, :, columns]

    over_heads(slots_ref.shape[2] // D_HEAD, 1, one_head)


def softmax_t(near, far, live):
    near = near * SCALING
    far = jnp.concatenate(
        [
            jnp.where(j < live, far[j * BLK : (j + 1) * BLK] * SCALING, -1e30)
            for j in range(NREM)
        ],
        axis=0,
    )
    highest = jnp.maximum(
        jnp.max(near, axis=0, keepdims=True), jnp.max(far, axis=0, keepdims=True)
    )
    near = jnp.exp(near - highest)
    far = jnp.exp(far - highest)
    total = jnp.sum(near, axis=0, keepdims=True) + jnp.sum(far, axis=0, keepdims=True)
    return near / total, far / total


def over_heads(head_count, unroll, body):
    @pl.loop(0, head_count // unroll)
    def _(i):
        for u in range(unroll):
            head = i * unroll + u
            body(head, pl.ds(pl.multiple_of(head * D_HEAD, D_HEAD), D_HEAD))


def value_kernel(me_ref, visible_ref, live_ref, q, do, k, *refs):
    key_refs, (dv, probs), out_refs, (k_slots, out_slots) = refs[:6], refs[6:8], refs[8:14], refs[14:]
    slots, lives = entries_of(me_ref, visible_ref, live_ref)
    clear(out_slots)
    fill(key_refs, k_slots)

    def one_head(head, columns):
        near_scores = dot_nt(k[:, columns], q[:, columns])
        near_probs = []
        for a in range(BLK_DEV):
            rows = slice(a * BLK, (a + 1) * BLK)
            far_k = jnp.concatenate([k_slots[s, :, columns] for s in slots[a]], axis=0)
            near_p, far_p = softmax_t(
                near_scores[:, rows], dot_nt(far_k, q[rows, columns]), lives[a]
            )
            near_probs.append(near_p.astype(jnp.bfloat16))
            far_p = far_p.astype(jnp.bfloat16)
            probs[head, BLK_DEV * BLK :, rows] = far_p
            far_term = dot(far_p, do[rows, columns]).astype(jnp.bfloat16)
            for j, s in enumerate(slots[a]):
                out_slots[s, :, columns] = far_term[j * BLK : (j + 1) * BLK]
        near_probs = jnp.concatenate(near_probs, axis=1)
        probs[head, : BLK_DEV * BLK, :] = near_probs
        dv[:, columns] = dot(near_probs, do[:, columns])

    over_heads(q.shape[1] // D_HEAD, 4, one_head)
    drain(out_slots, out_refs)


def key_kernel(me_ref, visible_ref, live_ref, q, do, probs, v, *refs):
    value_refs, ds, out_refs, (v_slots, out_slots) = refs[:6], refs[6], refs[7:13], refs[13:]
    slots, _ = entries_of(me_ref, visible_ref, live_ref)
    clear(out_slots)
    fill(value_refs, v_slots)

    def one_head(head, columns):
        near_grads = dot_nt(v[:, columns], do[:, columns])
        for a in range(BLK_DEV):
            rows = slice(a * BLK, (a + 1) * BLK)
            far_v = jnp.concatenate([v_slots[s, :, columns] for s in slots[a]], axis=0)
            near_g, far_g = near_grads[:, rows], dot_nt(far_v, do[rows, columns])
            near_p = probs[head, : BLK_DEV * BLK, rows].astype(jnp.float32)
            far_p = probs[head, BLK_DEV * BLK :, rows].astype(jnp.float32)
            delta = jnp.sum(near_p * near_g, axis=0, keepdims=True) + jnp.sum(
                far_p * far_g, axis=0, keepdims=True
            )
            ds[head, : BLK_DEV * BLK, rows] = (near_p * (near_g - delta) * SCALING).astype(
                jnp.bfloat16
            )
            far_ds = (far_p * (far_g - delta) * SCALING).astype(jnp.bfloat16)
            ds[head, BLK_DEV * BLK :, rows] = far_ds
            far_term = dot(far_ds, q[rows, columns]).astype(jnp.bfloat16)
            for j, s in enumerate(slots[a]):
                out_slots[s, :, columns] = far_term[j * BLK : (j + 1) * BLK]

    over_heads(q.shape[1] // D_HEAD, 4, one_head)
    drain(out_slots, out_refs)


def query_kernel(me_ref, visible_ref, live_ref, q, ds, k, *refs):
    key_refs, dq, dk, k_slots = refs[:6], refs[6], refs[7], refs[8]
    slots, _ = entries_of(me_ref, visible_ref, live_ref)
    fill(key_refs, k_slots)

    def one_head(head, columns):
        near_ds = ds[head, : BLK_DEV * BLK, :]
        near_dq = dot_tn(near_ds, k[:, columns])
        dk[:, columns] = dot(near_ds, q[:, columns])
        for a in range(BLK_DEV):
            rows = slice(a * BLK, (a + 1) * BLK)
            far_k = jnp.concatenate([k_slots[s, :, columns] for s in slots[a]], axis=0)
            far_dq = dot_tn(ds[head, BLK_DEV * BLK :, rows], far_k)
            dq[rows, columns] = (near_dq[rows] + far_dq).astype(jnp.bfloat16)

    over_heads(q.shape[1] // D_HEAD, 4, one_head)


def in_vmem(kernel, scalars, arrays, outs, scratch_count):
    width = arrays[0].shape[1]
    vmem = pl.BlockSpec(memory_space=pltpu.VMEM)
    return pl.pallas_call(
        kernel,
        out_shape=[
            jax.ShapeDtypeStruct(
                (width // D_HEAD, SEEN, rows[0]) if isinstance(rows, tuple) else (rows, width), kind
            )
            for rows, kind in outs
        ],
        in_specs=[pl.BlockSpec(memory_space=pltpu.SMEM)] * len(scalars) + [vmem] * len(arrays),
        out_specs=[vmem] * len(outs),
        scratch_shapes=[pltpu.VMEM((SLOTS, BLK, width), jnp.bfloat16)] * scratch_count,
        compiler_params=pltpu.CompilerParams(vmem_limit_bytes=32 * 1024 * 1024),
        cost_estimate=SMALL,
    )(*scalars, *arrays)


def dout_kernel(me_ref, weight, *refs):
    pieces, dout = refs[:-1], refs[-1]
    width = pieces[0].shape[1]
    total = None
    for d, piece in enumerate(pieces):
        columns = pl.ds(pl.multiple_of((me_ref[0] ^ d) * width, width), width)
        part = dot_nt(piece[...], weight[:, columns])
        total = part if total is None else total + part
    dout[...] = total.astype(jnp.bfloat16)


def project(tp_index, out_weight, pieces):
    rows, width = pieces[0].shape
    features = out_weight.shape[0]
    tile = min(256, features)
    return pl.pallas_call(
        dout_kernel,
        out_shape=jax.ShapeDtypeStruct((rows, features), jnp.bfloat16),
        grid_spec=pltpu.PrefetchScalarGridSpec(
            num_scalar_prefetch=1,
            grid=(features // tile,),
            in_specs=[pl.BlockSpec((tile, out_weight.shape[1]), lambda i, *_: (i, 0))]
            + [pl.BlockSpec((rows, width), lambda i, *_: (0, 0))] * len(pieces),
            out_specs=pl.BlockSpec((rows, tile), lambda i, *_: (0, i)),
        ),
        compiler_params=pltpu.CompilerParams(vmem_limit_bytes=32 * 1024 * 1024),
        cost_estimate=SMALL,
    )(tp_index.reshape(1), out_weight, *pieces)


def tied(*arrays):
    return lax.optimization_barrier(arrays)


def shards_cube(grad_out, out_weight, queries, keys, values, visible, live):
    myself = lax.axis_index("seq")
    row_count, feature_width = queries.shape
    other = myself ^ 1
    f32, bf16 = jnp.float32, jnp.bfloat16

    def hop(array, distance, axis="seq"):
        size = lax.axis_size(axis)
        return lax.ppermute(array, axis, [(i, i ^ distance) for i in range(size)])

    listed = lax.dynamic_slice_in_dim(visible, other * BLK_DEV, BLK_DEV, 0).reshape(-1)
    apart = (listed // BLK_DEV) ^ other
    wanted = [jnp.sum(jnp.where(apart == 2 * r + 1, listed % BLK_DEV, 0)) for r in range(CUBE // 2)]

    def pick(array, r):
        return lax.dynamic_slice_in_dim(array, wanted[r] * BLK, BLK, 0)

    def place(block, r):
        row = lax.broadcasted_iota(jnp.int32, (row_count, 1), 0) // BLK
        return jnp.where(row == wanted[r], jnp.concatenate([block, block], axis=0), 0).astype(f32)

    scalars = (myself.reshape(1), visible.reshape(-1), live)
    far_outs = [(2 * BLK, bf16)] * 4 + [(BLK, bf16)] * 2

    def stack(*blocks):
        return jnp.concatenate(blocks, axis=0)

    def sum_one(one, near):
        return (one.astype(f32) + place(near[BLK:], 1)).astype(bf16)

    def sum_three(three, far):
        return (three.astype(f32) + place(far, 3)).astype(bf16)

    def sum_two(two, x_two, three):
        return (two.astype(f32) + place(x_two, 2) + three.astype(f32)).astype(bf16)

    def total(near, x_near, one, two):
        return (near + place(x_near[:BLK], 0) + one.astype(f32) + two.astype(f32)).astype(bf16)

    k_two = hop(keys, 4)
    k_one = hop(keys, 2)
    pieces = [hop(grad_out, d, "tp") for d in range(lax.axis_size("tp") - 1, 0, -1)]
    k_one, k_two, values_b, keys_b = tied(k_one, k_two, values, keys)
    k_three = hop(k_two, 2)
    kx_near = hop(stack(pick(keys_b, 0), pick(k_one, 1)), 1)
    x_mixed = hop(stack(pick(k_two, 2), pick(values_b, 0)), 1)
    dout = project(lax.axis_index("tp"), out_weight, [grad_out, *pieces[::-1]])
    v_two = hop(values_b, 4)
    k_three, dout, values_b = tied(k_three, dout, values_b)
    kx_three = hop(pick(k_three, 3), 1)
    v_one = hop(values_b, 2)
    v_three = hop(v_two, 2)
    kx_three, v_two = tied(kx_three, v_two)
    vx_two = hop(pick(v_two, 2), 1)
    far_keys = (k_one, k_two, k_three, kx_near, x_mixed[:BLK], kx_three)
    dv, probs, dv_one, dv_two, dv_three, dvx_near, dvx_two, dvx_three = in_vmem(
        value_kernel, scalars, (queries, dout, keys, *far_keys),
        [(row_count, f32), ((row_count,), bf16)] + far_outs, 2,
    )
    dvx_three, dvx_two, v_one, v_three, vx_two = tied(
        hop(dvx_three, 1), dvx_two, v_one, v_three, vx_two
    )
    dv_three = hop(sum_three(dv_three, dvx_three), 2)
    vx_last = hop(stack(pick(v_one, 1), pick(v_three, 3)), 1)
    dvx_two = hop(dvx_two, 1)
    vx_last, dvx_near, dvx_two = tied(vx_last, dvx_near, dvx_two)
    dvx_near = hop(dvx_near, 1)
    far_values = (v_one, v_two, v_three, stack(x_mixed[BLK:], vx_last[:BLK]), vx_two, vx_last[BLK:])
    ds, dk_one, dk_two, dk_three, dkx_near, dkx_two, dkx_three = in_vmem(
        key_kernel, scalars, (queries, dout, probs, values, *far_values),
        [((row_count,), bf16)] + far_outs, 2,
    )
    dkx_three, dkx_two, dv_three, dvx_near = tied(dkx_three, dkx_two, dv_three, dvx_near)
    dv_two = hop(sum_two(dv_two, dvx_two, dv_three), 4)
    dv_one = hop(sum_one(dv_one, dvx_near), 2)
    dkx_three, dkx_two, dkx_near = tied(hop(dkx_three, 1), dkx_two, dkx_near)
    dk_three = hop(sum_three(dk_three, dkx_three), 2)
    dkx_two = hop(dkx_two, 1)
    dkx_near = hop(dkx_near, 1)
    dq, dk = in_vmem(
        query_kernel, scalars, (queries, ds, keys, *far_keys), [(row_count, bf16), (row_count, f32)], 1
    )
    dk_three, dkx_near, dv_two, dv_one, dq = tied(dk_three, dkx_near, dv_two, dv_one, dq)
    dk_two = hop(sum_two(dk_two, dkx_two, dk_three), 4)
    dk_one = hop(sum_one(dk_one, dkx_near), 2)
    grad_values = total(dv, dvx_near, dv_one, dv_two)
    grad_keys = total(dk, dkx_near, dk_one, dk_two)
    return (dq, grad_keys, grad_values)


def solution(mesh):
    placed = (
        P("seq", "tp"),
        P("tp", None),
        P("seq", "tp"),
        P("seq", "tp"),
        P("seq", "tp"),
        P(),
        P(),
    )
    return jax.shard_map(
        shards_cube if mesh.shape["seq"] == CUBE else shards_general,
        mesh=mesh,
        in_specs=placed,
        out_specs=(P("seq", "tp"), P("seq", "tp"), P("seq", "tp")),
        check_vma=False,
    )
```

```python
import functools
import math

import jax
import jax.numpy as jnp
from jax import lax
from jax.experimental import pallas as pl
from jax.experimental.pallas import tpu as pltpu
from jax.sharding import PartitionSpec as P

D_HEAD = 128
BLK = 128
BLK_DEV = 2
NREM = 3


def project_part(out_weight, piece):
    return lax.dot_general(
        piece, out_weight, (((1,), (1,)), ((), ())), preferred_element_type=jnp.float32
    )


def attend_group(query_group, dout_group, key_far, value_far, seen_mask, key_near, value_near):
    scaling = 1.0 / math.sqrt(D_HEAD)
    near_scores = (
        jnp.einsum("aihd,jhd->ahij", query_group, key_near, preferred_element_type=jnp.float32)
        * scaling
    )
    far_scores = (
        jnp.einsum("aihd,ajhd->ahij", query_group, key_far, preferred_element_type=jnp.float32)
        * scaling
    )
    far_scores = jnp.where(seen_mask[:, None, None, :], far_scores, -1e30)
    highest = jnp.maximum(jnp.max(near_scores, axis=3), jnp.max(far_scores, axis=3))[..., None]
    near_exp = jnp.exp(near_scores - highest)
    far_exp = jnp.exp(far_scores - highest)
    totals = jnp.sum(near_exp, axis=3, keepdims=True) + jnp.sum(far_exp, axis=3, keepdims=True)
    near_probs = near_exp / totals
    far_probs = far_exp / totals
    near_grad = jnp.einsum(
        "aihd,jhd->ahij", dout_group, value_near, preferred_element_type=jnp.float32
    )
    far_grad = jnp.einsum(
        "aihd,ajhd->ahij", dout_group, value_far, preferred_element_type=jnp.float32
    )
    row_delta = jnp.sum(near_probs * near_grad, axis=3, keepdims=True) + jnp.sum(
        far_probs * far_grad, axis=3, keepdims=True
    )
    near_ds = (near_probs * (near_grad - row_delta) * scaling).astype(jnp.bfloat16)
    far_ds = (far_probs * (far_grad - row_delta) * scaling).astype(jnp.bfloat16)
    grad_query = jnp.einsum("ahij,jhd->aihd", near_ds, key_near, preferred_element_type=jnp.float32)
    grad_query = grad_query + jnp.einsum(
        "ahij,ajhd->aihd", far_ds, key_far, preferred_element_type=jnp.float32
    )
    log_totals = (highest + jnp.log(totals))[..., 0]
    return (
        near_probs,
        far_probs,
        near_ds,
        far_ds,
        grad_query.astype(jnp.bfloat16),
        log_totals,
        row_delta[..., 0],
    )


def shards_general(grad_out, out_weight, queries, keys, values, visible, live):
    shard_count = lax.axis_size("seq")
    myself = lax.axis_index("seq")
    row_count, feature_width = queries.shape
    head_count = feature_width // D_HEAD
    entries = BLK_DEV * NREM
    capacity = min(BLK_DEV, -(-entries // (shard_count - 1)))
    slot_count = shard_count * capacity
    dout = project_part(out_weight, lax.all_gather(grad_out, "tp", axis=1, tiled=True)).astype(
        jnp.bfloat16
    )
    owners = (visible // BLK_DEV).reshape(shard_count, entries)
    block_within = (visible % BLK_DEV).reshape(shard_count, entries)
    living = (jnp.arange(NREM, dtype=jnp.int32)[None, :] < live[:, None]).reshape(
        shard_count, entries
    )
    positions = jnp.arange(entries, dtype=jnp.int32)
    earlier = positions[None, :] < positions[:, None]
    matching = (owners[:, :, None] == owners[:, None, :]) & living[:, None, :] & earlier[None, :, :]
    ranking = jnp.sum(matching.astype(jnp.int32), axis=2)
    slot_ids = jnp.arange(capacity, dtype=jnp.int32)
    chosen = (living & (owners == myself))[:, None, :] & (
        ranking[:, None, :] == slot_ids[None, :, None]
    )
    filled = jnp.any(chosen, axis=2).reshape(slot_count)
    send_index = jnp.sum(jnp.where(chosen, block_within[:, None, :], 0), axis=2).reshape(slot_count)
    key_blocks = keys.reshape(BLK_DEV, BLK, feature_width)
    value_blocks = values.reshape(BLK_DEV, BLK, feature_width)
    keep_slot = filled[:, None, None]
    send_keys = jnp.where(
        keep_slot, jnp.take(key_blocks, send_index, axis=0), jnp.zeros((), keys.dtype)
    )
    send_values = jnp.where(
        keep_slot, jnp.take(value_blocks, send_index, axis=0), jnp.zeros((), values.dtype)
    )
    fetched_keys, fetched_values = (
        lax.all_to_all(
            send_keys.reshape(shard_count, capacity, BLK, feature_width),
            "seq",
            split_axis=0,
            concat_axis=0,
            tiled=True,
        ),
        lax.all_to_all(
            send_values.reshape(shard_count, capacity, BLK, feature_width),
            "seq",
            split_axis=0,
            concat_axis=0,
            tiled=True,
        ),
    )
    my_owners = lax.dynamic_index_in_dim(owners, myself, 0, keepdims=False)
    my_ranks = lax.dynamic_index_in_dim(ranking, myself, 0, keepdims=False)
    my_living = lax.dynamic_index_in_dim(living, myself, 0, keepdims=False)
    fetch_index = my_owners * capacity + my_ranks
    key_far = jnp.take(fetched_keys.reshape(slot_count, BLK, feature_width), fetch_index, axis=0)
    value_far = jnp.take(
        fetched_values.reshape(slot_count, BLK, feature_width), fetch_index, axis=0
    )
    placement = (
        (jnp.arange(slot_count, dtype=jnp.int32)[:, None] == fetch_index[None, :])
        & my_living[None, :]
    ).astype(jnp.bfloat16)
    collect = (
        (jnp.arange(BLK_DEV, dtype=jnp.int32)[:, None] == send_index[None, :]) & filled[None, :]
    ).astype(jnp.bfloat16)
    group_size = math.gcd(BLK_DEV, max(1, 512 // BLK))
    group_count = BLK_DEV // group_size

    def grouped(array_in):
        return array_in.reshape((group_count, group_size) + array_in.shape[1:])

    query_blocks = grouped(queries.reshape(BLK_DEV, BLK, head_count, D_HEAD))
    dout_blocks = grouped(dout.reshape(BLK_DEV, BLK, head_count, D_HEAD))
    far_key_blocks = grouped(key_far.reshape(BLK_DEV, NREM * BLK, head_count, D_HEAD))
    far_value_blocks = grouped(value_far.reshape(BLK_DEV, NREM * BLK, head_count, D_HEAD))
    seen_blocks = grouped(jnp.repeat(my_living.reshape(BLK_DEV, NREM), BLK, axis=1))
    key_near = keys.reshape(row_count, head_count, D_HEAD)
    value_near = values.reshape(row_count, head_count, D_HEAD)

    def one_group(carry, inputs):
        near_key_acc, near_value_acc = carry
        query_group, dout_group, key_group, value_group, mask_group = inputs
        near_probs, far_probs, near_ds, far_ds, grad_query, log_totals, row_delta = attend_group(
            query_group, dout_group, key_group, value_group, mask_group, key_near, value_near
        )
        near_key_acc = near_key_acc + jnp.einsum(
            "ahij,aihd->jhd", near_ds, query_group, preferred_element_type=jnp.float32
        )
        near_value_acc = near_value_acc + jnp.einsum(
            "ahij,aihd->jhd",
            near_probs.astype(jnp.bfloat16),
            dout_group,
            preferred_element_type=jnp.float32,
        )
        far_key_term = jnp.einsum(
            "ahij,aihd->ajhd", far_ds, query_group, preferred_element_type=jnp.float32
        ).astype(jnp.bfloat16)
        far_value_term = jnp.einsum(
            "ahij,aihd->ajhd",
            far_probs.astype(jnp.bfloat16),
            dout_group,
            preferred_element_type=jnp.float32,
        ).astype(jnp.bfloat16)
        extra = (far_key_term, far_value_term)
        return ((near_key_acc, near_value_acc), (grad_query, extra))

    start = (
        jnp.zeros((row_count, head_count, D_HEAD), jnp.float32),
        jnp.zeros((row_count, head_count, D_HEAD), jnp.float32),
    )
    (near_keys, near_values), (grad_query_all, extra_all) = lax.scan(
        one_group, start, (query_blocks, dout_blocks, far_key_blocks, far_value_blocks, seen_blocks)
    )
    grad_queries = grad_query_all.reshape(row_count, feature_width)
    far_key_terms = extra_all[0].reshape(entries, BLK * feature_width)
    far_value_terms = extra_all[1].reshape(entries, BLK * feature_width)
    returned_keys = jnp.dot(placement, far_key_terms, preferred_element_type=jnp.float32).astype(
        jnp.bfloat16
    )
    returned_values = jnp.dot(
        placement, far_value_terms, preferred_element_type=jnp.float32
    ).astype(jnp.bfloat16)
    back_keys, back_values = (
        lax.all_to_all(
            returned_keys.reshape(shard_count, capacity, BLK, feature_width),
            "seq",
            split_axis=0,
            concat_axis=0,
            tiled=True,
        ),
        lax.all_to_all(
            returned_values.reshape(shard_count, capacity, BLK, feature_width),
            "seq",
            split_axis=0,
            concat_axis=0,
            tiled=True,
        ),
    )
    far_key_sum = jnp.dot(
        collect,
        back_keys.reshape(slot_count, BLK * feature_width),
        preferred_element_type=jnp.float32,
    )
    far_value_sum = jnp.dot(
        collect,
        back_values.reshape(slot_count, BLK * feature_width),
        preferred_element_type=jnp.float32,
    )
    grad_keys = (
        near_keys.reshape(row_count, feature_width) + far_key_sum.reshape(row_count, feature_width)
    ).astype(jnp.bfloat16)
    grad_values = (
        near_values.reshape(row_count, feature_width)
        + far_value_sum.reshape(row_count, feature_width)
    ).astype(jnp.bfloat16)
    return (grad_queries, grad_keys, grad_values)


CUBE = 8
SLOTS = 10
SEEN = (BLK_DEV + NREM) * BLK
SMALL = pl.CostEstimate(flops=1, bytes_accessed=1, transcendentals=0)
SCALING = 1.0 / math.sqrt(D_HEAD)


def slot_of(me, visible_ref, a, j):
    listed = visible_ref[(me * BLK_DEV + a) * NREM + j]
    apart = (listed // BLK_DEV) ^ me
    row = apart // 2
    return jnp.where(apart % 2 == 0, (row - 1) * BLK_DEV + listed % BLK_DEV, 6 + row)


def entries_of(me_ref, visible_ref, live_ref):
    me = me_ref[0]
    slots = [[slot_of(me, visible_ref, a, j) for j in range(NREM)] for a in range(BLK_DEV)]
    return slots, [live_ref[me * BLK_DEV + a] for a in range(BLK_DEV)]


def dot(a, b):
    return jnp.dot(a, b, preferred_element_type=jnp.float32)


def dot_nt(a, b):
    return lax.dot_general(a, b, (((1,), (1,)), ((), ())), preferred_element_type=jnp.float32)


def dot_tn(a, b):
    return lax.dot_general(a, b, (((0,), (0,)), ((), ())), preferred_element_type=jnp.float32)


def blocks_of(refs):
    return [(ref, i * BLK) for ref in refs for i in range(ref.shape[0] // BLK)]


def fill(refs, slots_ref):
    def one_head(head, columns):
        for at, (ref, row) in enumerate(blocks_of(refs)):
            slots_ref[at, :, columns] = ref[row : row + BLK, columns]

    over_heads(slots_ref.shape[2] // D_HEAD, 1, one_head)


def clear(slots_ref):
    def one_head(head, columns):
        for at in range(slots_ref.shape[0]):
            slots_ref[at, :, columns] = jnp.zeros((BLK, D_HEAD), slots_ref.dtype)

    over_heads(slots_ref.shape[2] // D_HEAD, 1, one_head)


def drain(slots_ref, refs):
    def one_head(head, columns):
        for at, (ref, row) in enumerate(blocks_of(refs)):
            ref[row : row + BLK, columns] = slots_ref[at, :, columns]

    over_heads(slots_ref.shape[2] // D_HEAD, 1, one_head)


def softmax_t(near, far, live):
    near = near * SCALING
    far = jnp.concatenate(
        [
            jnp.where(j < live, far[j * BLK : (j + 1) * BLK] * SCALING, -1e30)
            for j in range(NREM)
        ],
        axis=0,
    )
    highest = jnp.maximum(
        jnp.max(near, axis=0, keepdims=True), jnp.max(far, axis=0, keepdims=True)
    )
    near = jnp.exp(near - highest)
    far = jnp.exp(far - highest)
    total = jnp.sum(near, axis=0, keepdims=True) + jnp.sum(far, axis=0, keepdims=True)
    return near / total, far / total


def over_heads(head_count, unroll, body):
    @pl.loop(0, head_count // unroll)
    def _(i):
        for u in range(unroll):
            head = i * unroll + u
            body(head, pl.ds(pl.multiple_of(head * D_HEAD, D_HEAD), D_HEAD))


def value_kernel(me_ref, visible_ref, live_ref, q, do, k, *refs):
    key_refs, (dv, probs), out_refs, (k_slots, out_slots) = refs[:6], refs[6:8], refs[8:-2], refs[-2:]
    slots, lives = entries_of(me_ref, visible_ref, live_ref)
    clear(out_slots)
    fill(key_refs, k_slots)

    def one_head(head, columns):
        near_scores = dot_nt(k[:, columns], q[:, columns])
        near_probs = []
        for a in range(BLK_DEV):
            rows = slice(a * BLK, (a + 1) * BLK)
            far_k = jnp.concatenate([k_slots[s, :, columns] for s in slots[a]], axis=0)
            near_p, far_p = softmax_t(
                near_scores[:, rows], dot_nt(far_k, q[rows, columns]), lives[a]
            )
            near_probs.append(near_p.astype(jnp.bfloat16))
            far_p = far_p.astype(jnp.bfloat16)
            probs[head, BLK_DEV * BLK :, rows] = far_p
            far_term = dot(far_p, do[rows, columns]).astype(jnp.bfloat16)
            for j, s in enumerate(slots[a]):
                out_slots[s, :, columns] = far_term[j * BLK : (j + 1) * BLK]
        near_probs = jnp.concatenate(near_probs, axis=1)
        probs[head, : BLK_DEV * BLK, :] = near_probs
        dv[:, columns] = dot(near_probs, do[:, columns])

    over_heads(q.shape[1] // D_HEAD, 4, one_head)
    drain(out_slots, out_refs)


def key_kernel(first, me_ref, visible_ref, live_ref, q, do, probs, v, one, two, three, near, x_two, x_three, *refs):
    ds, out_refs, (v_slots, out_slots) = refs[0], refs[1:-2], refs[-2:]
    slots, _ = entries_of(me_ref, visible_ref, live_ref)
    clear(out_slots)
    fill((one, two, three, near, x_two, x_three), v_slots)

    def one_head(head, columns):
        whole = pl.ds(pl.multiple_of((first + head) * D_HEAD, D_HEAD), D_HEAD)
        near_grads = dot_nt(v[:, whole], do[:, whole])
        for a in range(BLK_DEV):
            rows = slice(a * BLK, (a + 1) * BLK)
            far_v = jnp.concatenate([v_slots[s, :, columns] for s in slots[a]], axis=0)
            near_g, far_g = near_grads[:, rows], dot_nt(far_v, do[rows, whole])
            near_p = probs[first + head, : BLK_DEV * BLK, rows].astype(jnp.float32)
            far_p = probs[first + head, BLK_DEV * BLK :, rows].astype(jnp.float32)
            delta = jnp.sum(near_p * near_g, axis=0, keepdims=True) + jnp.sum(
                far_p * far_g, axis=0, keepdims=True
            )
            ds[head, : BLK_DEV * BLK, rows] = (near_p * (near_g - delta) * SCALING).astype(
                jnp.bfloat16
            )
            far_ds = (far_p * (far_g - delta) * SCALING).astype(jnp.bfloat16)
            ds[head, BLK_DEV * BLK :, rows] = far_ds
            far_term = dot(far_ds, q[rows, whole]).astype(jnp.bfloat16)
            for j, s in enumerate(slots[a]):
                out_slots[s, :, columns] = far_term[j * BLK : (j + 1) * BLK]

    over_heads(ds.shape[0], 4, one_head)
    drain(out_slots, out_refs)


def query_kernel(me_ref, visible_ref, live_ref, q, ds, k, *refs):
    key_refs, dq, dk, k_slots = refs[:6], refs[6], refs[7], refs[8]
    slots, _ = entries_of(me_ref, visible_ref, live_ref)
    fill(key_refs, k_slots)

    def one_head(head, columns):
        near_ds = ds[head, : BLK_DEV * BLK, :]
        near_dq = dot_tn(near_ds, k[:, columns])
        dk[:, columns] = dot(near_ds, q[:, columns])
        for a in range(BLK_DEV):
            rows = slice(a * BLK, (a + 1) * BLK)
            far_k = jnp.concatenate([k_slots[s, :, columns] for s in slots[a]], axis=0)
            far_dq = dot_tn(ds[head, BLK_DEV * BLK :, rows], far_k)
            dq[rows, columns] = (near_dq[rows] + far_dq).astype(jnp.bfloat16)

    over_heads(q.shape[1] // D_HEAD, 4, one_head)


def in_vmem(kernel, scalars, arrays, outs, scratch_count, width):
    vmem = pl.BlockSpec(memory_space=pltpu.VMEM)
    return pl.pallas_call(
        kernel,
        out_shape=[
            jax.ShapeDtypeStruct(
                (width // D_HEAD, SEEN, rows[0]) if isinstance(rows, tuple) else (rows, width), kind
            )
            for rows, kind in outs
        ],
        in_specs=[pl.BlockSpec(memory_space=pltpu.SMEM)] * len(scalars) + [vmem] * len(arrays),
        out_specs=[vmem] * len(outs),
        scratch_shapes=[pltpu.VMEM((SLOTS, BLK, width), jnp.bfloat16)] * scratch_count,
        compiler_params=pltpu.CompilerParams(vmem_limit_bytes=32 * 1024 * 1024),
        cost_estimate=SMALL,
    )(*scalars, *arrays)


def dout_kernel(me_ref, weight, *refs):
    pieces, dout = refs[:-1], refs[-1]
    width = pieces[0].shape[1]
    total = None
    for d, piece in enumerate(pieces):
        columns = pl.ds(pl.multiple_of((me_ref[0] ^ d) * width, width), width)
        part = dot_nt(piece[...], weight[:, columns])
        total = part if total is None else total + part
    dout[...] = total.astype(jnp.bfloat16)


def project(tp_index, out_weight, pieces):
    rows, width = pieces[0].shape
    features = out_weight.shape[0]
    tile = min(256, features)
    return pl.pallas_call(
        dout_kernel,
        out_shape=jax.ShapeDtypeStruct((rows, features), jnp.bfloat16),
        grid_spec=pltpu.PrefetchScalarGridSpec(
            num_scalar_prefetch=1,
            grid=(features // tile,),
            in_specs=[pl.BlockSpec((tile, out_weight.shape[1]), lambda i, *_: (i, 0))]
            + [pl.BlockSpec((rows, width), lambda i, *_: (0, 0))] * len(pieces),
            out_specs=pl.BlockSpec((rows, tile), lambda i, *_: (0, i)),
        ),
        compiler_params=pltpu.CompilerParams(vmem_limit_bytes=32 * 1024 * 1024),
        cost_estimate=SMALL,
    )(tp_index.reshape(1), out_weight, *pieces)


def tied(*arrays):
    return lax.optimization_barrier(arrays)


def shards_cube(grad_out, out_weight, queries, keys, values, visible, live):
    myself = lax.axis_index("seq")
    row_count, feature_width = queries.shape
    other = myself ^ 1
    f32, bf16 = jnp.float32, jnp.bfloat16

    def hop(array, distance, axis="seq"):
        size = lax.axis_size(axis)
        return lax.ppermute(array, axis, [(i, i ^ distance) for i in range(size)])

    listed = lax.dynamic_slice_in_dim(visible, other * BLK_DEV, BLK_DEV, 0).reshape(-1)
    apart = (listed // BLK_DEV) ^ other
    wanted = [jnp.sum(jnp.where(apart == 2 * r + 1, listed % BLK_DEV, 0)) for r in range(CUBE // 2)]

    def pick(array, r):
        return lax.dynamic_slice_in_dim(array, wanted[r] * BLK, BLK, 0)

    def place(block, r):
        row = lax.broadcasted_iota(jnp.int32, (row_count, 1), 0) // BLK
        return jnp.where(row == wanted[r], jnp.concatenate([block, block], axis=0), 0).astype(f32)

    scalars = (myself.reshape(1), visible.reshape(-1), live)
    far_outs = [(2 * BLK, bf16)] * 3

    def stack(*blocks):
        return jnp.concatenate(blocks, axis=0)

    def sum_one(one, x_one):
        return (one.astype(f32) + place(x_one, 1)).astype(bf16)

    def sum_three(three, far):
        return (three.astype(f32) + place(far, 3)).astype(bf16)

    def sum_two(two, x_two, three):
        return (two.astype(f32) + place(x_two, 2) + three.astype(f32)).astype(bf16)

    def total(near, x_own, one, two):
        return (near + place(x_own, 0) + one.astype(f32) + two.astype(f32)).astype(bf16)

    k_two = hop(keys, 4)
    k_one = hop(keys, 2)
    pieces = [hop(grad_out, d, "tp") for d in range(lax.axis_size("tp") - 1, 0, -1)]
    pieces[-1], keys_b, values_b = tied(pieces[-1], keys, values)
    x_own = hop(stack(pick(keys_b, 0), pick(values_b, 0)), 1)
    k_one, k_two, values_b, x_own = tied(k_one, k_two, values_b, x_own)
    k_three = hop(k_two, 2)
    kx_near = hop(stack(pick(k_one, 1), pick(k_two, 2)), 1)
    dout = project(lax.axis_index("tp"), out_weight, [grad_out, *pieces[::-1]])
    dout, values_b = tied(dout, values_b)
    v_two = hop(values_b, 4)
    k_three, kx_near, x_own, values_b = tied(k_three, kx_near, x_own, values_b)
    v_one = hop(values_b, 2)
    kx_three = hop(pick(k_three, 3), 1)
    far_keys = (k_one, k_two, k_three, stack(x_own[:BLK], kx_near[:BLK]), kx_near[BLK:], kx_three)
    dv, probs, dv_one, dv_two, dv_three, dvx_own, dvx_one, dvx_two, dvx_three = in_vmem(
        value_kernel, scalars, (queries, dout, keys, *far_keys),
        [(row_count, f32), ((row_count,), bf16)] + far_outs + [(BLK, bf16)] * 4, 2, feature_width,
    )
    dvx_three = hop(dvx_three, 1)
    dvx_one = hop(dvx_one, 1)
    v_two, v_one, dvx_two, dvx_three, dvx_one = tied(v_two, v_one, dvx_two, dvx_three, dvx_one)
    v_three = hop(v_two, 2)
    vx_near = hop(stack(pick(v_one, 1), pick(v_two, 2)), 1)
    v_three, dv_three, dv_one = tied(
        v_three, sum_three(dv_three, dvx_three), sum_one(dv_one, dvx_one)
    )
    vx_three = hop(pick(v_three, 3), 1)
    dv_three = hop(dv_three, 2)
    dv_one = hop(dv_one, 2)
    vx_three, vx_near, dvx_two = tied(vx_three, vx_near, dvx_two)
    dvx_two = hop(dvx_two, 1)
    ds, dk_one, dk_two, dk_three, dkx_own, dkx_near, dkx_three = in_vmem(
        functools.partial(key_kernel, 0), scalars,
        (queries, dout, probs, values, v_one, v_two, v_three,
         stack(x_own[BLK:], vx_near[:BLK]), vx_near[BLK:], vx_three),
        [((row_count,), bf16)] + far_outs + [(BLK, bf16), (2 * BLK, bf16), (BLK, bf16)],
        2, feature_width,
    )
    dkx_three, dv_three, dkx_near, dvx_two = tied(dkx_three, dv_three, dkx_near, dvx_two)
    dkx_three = hop(dkx_three, 1)
    dv_two = hop(sum_two(dv_two, dvx_two, dv_three), 4)
    dkx_three, dkx_near, dv_one = tied(dkx_three, dkx_near, dv_one)
    dk_three = hop(sum_three(dk_three, dkx_three), 2)
    dkx_near = hop(dkx_near, 1)
    dq, dk = in_vmem(
        query_kernel, scalars, (queries, ds, keys, *far_keys),
        [(row_count, bf16), (row_count, f32)], 1, feature_width,
    )
    dk_three, dkx_near, dq, dv_two = tied(dk_three, dkx_near, dq, dv_two)
    dk_two = hop(sum_two(dk_two, dkx_near[BLK:], dk_three), 4)
    dk_one = hop(sum_one(dk_one, dkx_near[:BLK]), 2)
    x_own = hop(stack(dvx_own, dkx_own), 1)
    grad_values = total(dv, x_own[:BLK], dv_one, dv_two)
    grad_keys = total(dk, x_own[BLK:], dk_one, dk_two)
    return (dq, grad_keys, grad_values)


def solution(mesh):
    placed = (
        P("seq", "tp"),
        P("tp", None),
        P("seq", "tp"),
        P("seq", "tp"),
        P("seq", "tp"),
        P(),
        P(),
    )
    return jax.shard_map(
        shards_cube if mesh.shape["seq"] == CUBE else shards_general,
        mesh=mesh,
        in_specs=placed,
        out_specs=(P("seq", "tp"), P("seq", "tp"), P("seq", "tp")),
        check_vma=False,
    )
```

```python
import functools
import math

import jax
import jax.numpy as jnp
from jax import lax
from jax.experimental import pallas as pl
from jax.experimental.pallas import tpu as pltpu
from jax.sharding import PartitionSpec as P

D_HEAD = 128
BLK = 128
BLK_DEV = 2
NREM = 3


def project_part(out_weight, piece):
    return lax.dot_general(
        piece, out_weight, (((1,), (1,)), ((), ())), preferred_element_type=jnp.float32
    )


def attend_group(query_group, dout_group, key_far, value_far, seen_mask, key_near, value_near):
    scaling = 1.0 / math.sqrt(D_HEAD)
    near_scores = (
        jnp.einsum("aihd,jhd->ahij", query_group, key_near, preferred_element_type=jnp.float32)
        * scaling
    )
    far_scores = (
        jnp.einsum("aihd,ajhd->ahij", query_group, key_far, preferred_element_type=jnp.float32)
        * scaling
    )
    far_scores = jnp.where(seen_mask[:, None, None, :], far_scores, -1e30)
    highest = jnp.maximum(jnp.max(near_scores, axis=3), jnp.max(far_scores, axis=3))[..., None]
    near_exp = jnp.exp(near_scores - highest)
    far_exp = jnp.exp(far_scores - highest)
    totals = jnp.sum(near_exp, axis=3, keepdims=True) + jnp.sum(far_exp, axis=3, keepdims=True)
    near_probs = near_exp / totals
    far_probs = far_exp / totals
    near_grad = jnp.einsum(
        "aihd,jhd->ahij", dout_group, value_near, preferred_element_type=jnp.float32
    )
    far_grad = jnp.einsum(
        "aihd,ajhd->ahij", dout_group, value_far, preferred_element_type=jnp.float32
    )
    row_delta = jnp.sum(near_probs * near_grad, axis=3, keepdims=True) + jnp.sum(
        far_probs * far_grad, axis=3, keepdims=True
    )
    near_ds = (near_probs * (near_grad - row_delta) * scaling).astype(jnp.bfloat16)
    far_ds = (far_probs * (far_grad - row_delta) * scaling).astype(jnp.bfloat16)
    grad_query = jnp.einsum("ahij,jhd->aihd", near_ds, key_near, preferred_element_type=jnp.float32)
    grad_query = grad_query + jnp.einsum(
        "ahij,ajhd->aihd", far_ds, key_far, preferred_element_type=jnp.float32
    )
    log_totals = (highest + jnp.log(totals))[..., 0]
    return (
        near_probs,
        far_probs,
        near_ds,
        far_ds,
        grad_query.astype(jnp.bfloat16),
        log_totals,
        row_delta[..., 0],
    )


def shards_general(grad_out, out_weight, queries, keys, values, visible, live):
    shard_count = lax.axis_size("seq")
    myself = lax.axis_index("seq")
    row_count, feature_width = queries.shape
    head_count = feature_width // D_HEAD
    entries = BLK_DEV * NREM
    capacity = min(BLK_DEV, -(-entries // (shard_count - 1)))
    slot_count = shard_count * capacity
    dout = project_part(out_weight, lax.all_gather(grad_out, "tp", axis=1, tiled=True)).astype(
        jnp.bfloat16
    )
    owners = (visible // BLK_DEV).reshape(shard_count, entries)
    block_within = (visible % BLK_DEV).reshape(shard_count, entries)
    living = (jnp.arange(NREM, dtype=jnp.int32)[None, :] < live[:, None]).reshape(
        shard_count, entries
    )
    positions = jnp.arange(entries, dtype=jnp.int32)
    earlier = positions[None, :] < positions[:, None]
    matching = (owners[:, :, None] == owners[:, None, :]) & living[:, None, :] & earlier[None, :, :]
    ranking = jnp.sum(matching.astype(jnp.int32), axis=2)
    slot_ids = jnp.arange(capacity, dtype=jnp.int32)
    chosen = (living & (owners == myself))[:, None, :] & (
        ranking[:, None, :] == slot_ids[None, :, None]
    )
    filled = jnp.any(chosen, axis=2).reshape(slot_count)
    send_index = jnp.sum(jnp.where(chosen, block_within[:, None, :], 0), axis=2).reshape(slot_count)
    key_blocks = keys.reshape(BLK_DEV, BLK, feature_width)
    value_blocks = values.reshape(BLK_DEV, BLK, feature_width)
    keep_slot = filled[:, None, None]
    send_keys = jnp.where(
        keep_slot, jnp.take(key_blocks, send_index, axis=0), jnp.zeros((), keys.dtype)
    )
    send_values = jnp.where(
        keep_slot, jnp.take(value_blocks, send_index, axis=0), jnp.zeros((), values.dtype)
    )
    fetched_keys, fetched_values = (
        lax.all_to_all(
            send_keys.reshape(shard_count, capacity, BLK, feature_width),
            "seq",
            split_axis=0,
            concat_axis=0,
            tiled=True,
        ),
        lax.all_to_all(
            send_values.reshape(shard_count, capacity, BLK, feature_width),
            "seq",
            split_axis=0,
            concat_axis=0,
            tiled=True,
        ),
    )
    my_owners = lax.dynamic_index_in_dim(owners, myself, 0, keepdims=False)
    my_ranks = lax.dynamic_index_in_dim(ranking, myself, 0, keepdims=False)
    my_living = lax.dynamic_index_in_dim(living, myself, 0, keepdims=False)
    fetch_index = my_owners * capacity + my_ranks
    key_far = jnp.take(fetched_keys.reshape(slot_count, BLK, feature_width), fetch_index, axis=0)
    value_far = jnp.take(
        fetched_values.reshape(slot_count, BLK, feature_width), fetch_index, axis=0
    )
    placement = (
        (jnp.arange(slot_count, dtype=jnp.int32)[:, None] == fetch_index[None, :])
        & my_living[None, :]
    ).astype(jnp.bfloat16)
    collect = (
        (jnp.arange(BLK_DEV, dtype=jnp.int32)[:, None] == send_index[None, :]) & filled[None, :]
    ).astype(jnp.bfloat16)
    group_size = math.gcd(BLK_DEV, max(1, 512 // BLK))
    group_count = BLK_DEV // group_size

    def grouped(array_in):
        return array_in.reshape((group_count, group_size) + array_in.shape[1:])

    query_blocks = grouped(queries.reshape(BLK_DEV, BLK, head_count, D_HEAD))
    dout_blocks = grouped(dout.reshape(BLK_DEV, BLK, head_count, D_HEAD))
    far_key_blocks = grouped(key_far.reshape(BLK_DEV, NREM * BLK, head_count, D_HEAD))
    far_value_blocks = grouped(value_far.reshape(BLK_DEV, NREM * BLK, head_count, D_HEAD))
    seen_blocks = grouped(jnp.repeat(my_living.reshape(BLK_DEV, NREM), BLK, axis=1))
    key_near = keys.reshape(row_count, head_count, D_HEAD)
    value_near = values.reshape(row_count, head_count, D_HEAD)

    def one_group(carry, inputs):
        near_key_acc, near_value_acc = carry
        query_group, dout_group, key_group, value_group, mask_group = inputs
        near_probs, far_probs, near_ds, far_ds, grad_query, log_totals, row_delta = attend_group(
            query_group, dout_group, key_group, value_group, mask_group, key_near, value_near
        )
        near_key_acc = near_key_acc + jnp.einsum(
            "ahij,aihd->jhd", near_ds, query_group, preferred_element_type=jnp.float32
        )
        near_value_acc = near_value_acc + jnp.einsum(
            "ahij,aihd->jhd",
            near_probs.astype(jnp.bfloat16),
            dout_group,
            preferred_element_type=jnp.float32,
        )
        far_key_term = jnp.einsum(
            "ahij,aihd->ajhd", far_ds, query_group, preferred_element_type=jnp.float32
        ).astype(jnp.bfloat16)
        far_value_term = jnp.einsum(
            "ahij,aihd->ajhd",
            far_probs.astype(jnp.bfloat16),
            dout_group,
            preferred_element_type=jnp.float32,
        ).astype(jnp.bfloat16)
        extra = (far_key_term, far_value_term)
        return ((near_key_acc, near_value_acc), (grad_query, extra))

    start = (
        jnp.zeros((row_count, head_count, D_HEAD), jnp.float32),
        jnp.zeros((row_count, head_count, D_HEAD), jnp.float32),
    )
    (near_keys, near_values), (grad_query_all, extra_all) = lax.scan(
        one_group, start, (query_blocks, dout_blocks, far_key_blocks, far_value_blocks, seen_blocks)
    )
    grad_queries = grad_query_all.reshape(row_count, feature_width)
    far_key_terms = extra_all[0].reshape(entries, BLK * feature_width)
    far_value_terms = extra_all[1].reshape(entries, BLK * feature_width)
    returned_keys = jnp.dot(placement, far_key_terms, preferred_element_type=jnp.float32).astype(
        jnp.bfloat16
    )
    returned_values = jnp.dot(
        placement, far_value_terms, preferred_element_type=jnp.float32
    ).astype(jnp.bfloat16)
    back_keys, back_values = (
        lax.all_to_all(
            returned_keys.reshape(shard_count, capacity, BLK, feature_width),
            "seq",
            split_axis=0,
            concat_axis=0,
            tiled=True,
        ),
        lax.all_to_all(
            returned_values.reshape(shard_count, capacity, BLK, feature_width),
            "seq",
            split_axis=0,
            concat_axis=0,
            tiled=True,
        ),
    )
    far_key_sum = jnp.dot(
        collect,
        back_keys.reshape(slot_count, BLK * feature_width),
        preferred_element_type=jnp.float32,
    )
    far_value_sum = jnp.dot(
        collect,
        back_values.reshape(slot_count, BLK * feature_width),
        preferred_element_type=jnp.float32,
    )
    grad_keys = (
        near_keys.reshape(row_count, feature_width) + far_key_sum.reshape(row_count, feature_width)
    ).astype(jnp.bfloat16)
    grad_values = (
        near_values.reshape(row_count, feature_width)
        + far_value_sum.reshape(row_count, feature_width)
    ).astype(jnp.bfloat16)
    return (grad_queries, grad_keys, grad_values)


CUBE = 8
SLOTS = 10
VMEM_LIMIT = 14 * 1024 * 1024
SEEN = (BLK_DEV + NREM) * BLK
SMALL = pl.CostEstimate(flops=1, bytes_accessed=1, transcendentals=0)
SCALING = 1.0 / math.sqrt(D_HEAD)


def slot_of(me, visible_ref, a, j):
    listed = visible_ref[(me * BLK_DEV + a) * NREM + j]
    apart = (listed // BLK_DEV) ^ me
    row = apart // 2
    return jnp.where(apart % 2 == 0, (row - 1) * BLK_DEV + listed % BLK_DEV, 6 + row)


def entries_of(me_ref, visible_ref, live_ref):
    me = me_ref[0]
    slots = [[slot_of(me, visible_ref, a, j) for j in range(NREM)] for a in range(BLK_DEV)]
    return slots, [live_ref[me * BLK_DEV + a] for a in range(BLK_DEV)]


def dot(a, b):
    return jnp.dot(a, b, preferred_element_type=jnp.float32)


def dot_nt(a, b):
    return lax.dot_general(a, b, (((1,), (1,)), ((), ())), preferred_element_type=jnp.float32)


def dot_tn(a, b):
    return lax.dot_general(a, b, (((0,), (0,)), ((), ())), preferred_element_type=jnp.float32)


def blocks_of(refs):
    return [(ref, i * BLK) for ref in refs for i in range(ref.shape[0] // BLK)]


def fill(refs, slots_ref):
    def one_head(head, columns):
        for at, (ref, row) in enumerate(blocks_of(refs)):
            slots_ref[at, :, columns] = ref[row : row + BLK, columns]

    over_heads(slots_ref.shape[2] // D_HEAD, 1, one_head)


def clear(slots_ref):
    def one_head(head, columns):
        for at in range(slots_ref.shape[0]):
            slots_ref[at, :, columns] = jnp.zeros((BLK, D_HEAD), slots_ref.dtype)

    over_heads(slots_ref.shape[2] // D_HEAD, 1, one_head)


def drain(slots_ref, refs):
    def one_head(head, columns):
        for at, (ref, row) in enumerate(blocks_of(refs)):
            ref[row : row + BLK, columns] = slots_ref[at, :, columns]

    over_heads(slots_ref.shape[2] // D_HEAD, 1, one_head)


def softmax_t(near, far, live):
    near = near * SCALING
    far = jnp.concatenate(
        [
            jnp.where(j < live, far[j * BLK : (j + 1) * BLK] * SCALING, -1e30)
            for j in range(NREM)
        ],
        axis=0,
    )
    highest = jnp.maximum(
        jnp.max(near, axis=0, keepdims=True), jnp.max(far, axis=0, keepdims=True)
    )
    near = jnp.exp(near - highest)
    far = jnp.exp(far - highest)
    total = jnp.sum(near, axis=0, keepdims=True) + jnp.sum(far, axis=0, keepdims=True)
    return near / total, far / total


def over_heads(head_count, unroll, body):
    @pl.loop(0, head_count // unroll)
    def _(i):
        for u in range(unroll):
            head = i * unroll + u
            body(head, pl.ds(pl.multiple_of(head * D_HEAD, D_HEAD), D_HEAD))


def value_kernel(me_ref, visible_ref, live_ref, q, do, k, *refs):
    key_refs, (dv, probs), out_refs, (k_slots, out_slots) = refs[:6], refs[6:8], refs[8:-2], refs[-2:]
    slots, lives = entries_of(me_ref, visible_ref, live_ref)
    clear(out_slots)
    fill(key_refs, k_slots)

    def one_head(head, columns):
        near_scores = dot_nt(k[:, columns], q[:, columns])
        near_probs = []
        for a in range(BLK_DEV):
            rows = slice(a * BLK, (a + 1) * BLK)
            far_k = jnp.concatenate([k_slots[s, :, columns] for s in slots[a]], axis=0)
            near_p, far_p = softmax_t(
                near_scores[:, rows], dot_nt(far_k, q[rows, columns]), lives[a]
            )
            near_probs.append(near_p.astype(jnp.bfloat16))
            far_p = far_p.astype(jnp.bfloat16)
            probs[head, BLK_DEV * BLK :, rows] = far_p
            far_term = dot(far_p, do[rows, columns]).astype(jnp.bfloat16)
            for j, s in enumerate(slots[a]):
                out_slots[s, :, columns] = far_term[j * BLK : (j + 1) * BLK]
        near_probs = jnp.concatenate(near_probs, axis=1)
        probs[head, : BLK_DEV * BLK, :] = near_probs
        dv[:, columns] = dot(near_probs, do[:, columns])

    over_heads(q.shape[1] // D_HEAD, 4, one_head)
    drain(out_slots, out_refs)


def key_kernel(first, me_ref, visible_ref, live_ref, q, do, probs, v, one, two, three, near, x_two, x_three, *refs):
    ds, out_refs, (v_slots, out_slots) = refs[0], refs[1:-2], refs[-2:]
    slots, _ = entries_of(me_ref, visible_ref, live_ref)
    clear(out_slots)
    fill((one, two, three, near, x_two, x_three), v_slots)

    def one_head(head, columns):
        whole = pl.ds(pl.multiple_of((first + head) * D_HEAD, D_HEAD), D_HEAD)
        near_grads = dot_nt(v[:, whole], do[:, whole])
        for a in range(BLK_DEV):
            rows = slice(a * BLK, (a + 1) * BLK)
            far_v = jnp.concatenate([v_slots[s, :, columns] for s in slots[a]], axis=0)
            near_g, far_g = near_grads[:, rows], dot_nt(far_v, do[rows, whole])
            near_p = probs[first + head, : BLK_DEV * BLK, rows].astype(jnp.float32)
            far_p = probs[first + head, BLK_DEV * BLK :, rows].astype(jnp.float32)
            delta = jnp.sum(near_p * near_g, axis=0, keepdims=True) + jnp.sum(
                far_p * far_g, axis=0, keepdims=True
            )
            ds[head, : BLK_DEV * BLK, rows] = (near_p * (near_g - delta) * SCALING).astype(
                jnp.bfloat16
            )
            far_ds = (far_p * (far_g - delta) * SCALING).astype(jnp.bfloat16)
            ds[head, BLK_DEV * BLK :, rows] = far_ds
            far_term = dot(far_ds, q[rows, whole]).astype(jnp.bfloat16)
            for j, s in enumerate(slots[a]):
                out_slots[s, :, columns] = far_term[j * BLK : (j + 1) * BLK]

    over_heads(ds.shape[0], 4, one_head)
    drain(out_slots, out_refs)


def query_kernel(me_ref, visible_ref, live_ref, q, ds, k, *refs):
    key_refs, dq, dk, k_slots = refs[:6], refs[6], refs[7], refs[8]
    slots, _ = entries_of(me_ref, visible_ref, live_ref)
    fill(key_refs, k_slots)

    def one_head(head, columns):
        near_ds = ds[head, : BLK_DEV * BLK, :]
        near_dq = dot_tn(near_ds, k[:, columns])
        dk[:, columns] = dot(near_ds, q[:, columns])
        for a in range(BLK_DEV):
            rows = slice(a * BLK, (a + 1) * BLK)
            far_k = jnp.concatenate([k_slots[s, :, columns] for s in slots[a]], axis=0)
            far_dq = dot_tn(ds[head, BLK_DEV * BLK :, rows], far_k)
            dq[rows, columns] = (near_dq[rows] + far_dq).astype(jnp.bfloat16)

    over_heads(q.shape[1] // D_HEAD, 4, one_head)


def in_vmem(kernel, scalars, arrays, outs, scratch_count, width):
    vmem = pl.BlockSpec(memory_space=pltpu.VMEM)
    return pl.pallas_call(
        kernel,
        out_shape=[
            jax.ShapeDtypeStruct(
                (width // D_HEAD, SEEN, rows[0]) if isinstance(rows, tuple) else (rows, width), kind
            )
            for rows, kind in outs
        ],
        in_specs=[pl.BlockSpec(memory_space=pltpu.SMEM)] * len(scalars) + [vmem] * len(arrays),
        out_specs=[vmem] * len(outs),
        scratch_shapes=[pltpu.VMEM((SLOTS, BLK, width), jnp.bfloat16)] * scratch_count,
        compiler_params=pltpu.CompilerParams(vmem_limit_bytes=VMEM_LIMIT),
        cost_estimate=SMALL,
    )(*scalars, *arrays)


def dout_kernel(me_ref, weight, *refs):
    pieces, dout = refs[:-1], refs[-1]
    width = pieces[0].shape[1]
    total = None
    for d, piece in enumerate(pieces):
        columns = pl.ds(pl.multiple_of((me_ref[0] ^ d) * width, width), width)
        part = dot_nt(piece[...], weight[:, columns])
        total = part if total is None else total + part
    dout[...] = total.astype(jnp.bfloat16)


def project(tp_index, out_weight, pieces):
    rows, width = pieces[0].shape
    features = out_weight.shape[0]
    tile = min(256, features)
    return pl.pallas_call(
        dout_kernel,
        out_shape=jax.ShapeDtypeStruct((rows, features), jnp.bfloat16),
        grid_spec=pltpu.PrefetchScalarGridSpec(
            num_scalar_prefetch=1,
            grid=(features // tile,),
            in_specs=[pl.BlockSpec((tile, out_weight.shape[1]), lambda i, *_: (i, 0))]
            + [pl.BlockSpec((rows, width), lambda i, *_: (0, 0))] * len(pieces),
            out_specs=pl.BlockSpec((rows, tile), lambda i, *_: (0, i)),
        ),
        compiler_params=pltpu.CompilerParams(vmem_limit_bytes=VMEM_LIMIT),
        cost_estimate=SMALL,
    )(tp_index.reshape(1), out_weight, *pieces)


def tied(*arrays):
    return lax.optimization_barrier(arrays)


def shards_cube(grad_out, out_weight, queries, keys, values, visible, live):
    myself = lax.axis_index("seq")
    row_count, feature_width = queries.shape
    other = myself ^ 1
    f32, bf16 = jnp.float32, jnp.bfloat16

    def hop(array, distance, axis="seq"):
        size = lax.axis_size(axis)
        return lax.ppermute(array, axis, [(i, i ^ distance) for i in range(size)])

    listed = lax.dynamic_slice_in_dim(visible, other * BLK_DEV, BLK_DEV, 0).reshape(-1)
    apart = (listed // BLK_DEV) ^ other
    wanted = [jnp.sum(jnp.where(apart == 2 * r + 1, listed % BLK_DEV, 0)) for r in range(CUBE // 2)]

    def pick(array, r):
        return lax.dynamic_slice_in_dim(array, wanted[r] * BLK, BLK, 0)

    def place(block, r):
        row = lax.broadcasted_iota(jnp.int32, (row_count, 1), 0) // BLK
        return jnp.where(row == wanted[r], jnp.concatenate([block, block], axis=0), 0).astype(f32)

    scalars = (myself.reshape(1), visible.reshape(-1), live)
    far_outs = [(2 * BLK, bf16)] * 3

    def stack(*blocks):
        return jnp.concatenate(blocks, axis=0)

    def sum_one(one, x_one):
        return (one.astype(f32) + place(x_one, 1)).astype(bf16)

    def sum_three(three, far):
        return (three.astype(f32) + place(far, 3)).astype(bf16)

    def sum_two(two, x_two, three):
        return (two.astype(f32) + place(x_two, 2) + three.astype(f32)).astype(bf16)

    def total(near, x_own, one, two):
        return (near + place(x_own, 0) + one.astype(f32) + two.astype(f32)).astype(bf16)

    at_end = (myself // 2 == 0) | (myself // 2 == 3)

    def across(array):
        ends = [(i, i) for i in (0, 1, 6, 7)]
        return lax.ppermute(array, "seq", ends + [(2, 4), (3, 5), (4, 2), (5, 3)])

    k_two = hop(keys, 4)
    k_one = hop(keys, 2)
    pieces = [hop(grad_out, d, "tp") for d in range(lax.axis_size("tp") - 1, 0, -1)]
    pieces[-1], keys_b, values_b, at_end = tied(pieces[-1], keys, values, at_end)
    x_own = hop(stack(pick(keys_b, 0), pick(values_b, 0)), 1)
    k_one, k_two, values_b, x_own = tied(k_one, k_two, values_b, x_own)
    k_three = hop(k_two, 2)
    v_across = across(values_b)
    kx_near = hop(stack(pick(k_one, 1), pick(k_two, 2)), 1)
    k_three, values_b, v_across, *pieces = tied(k_three, values_b, v_across, *pieces)
    v_two = hop(values_b, 4)
    v_one = hop(values_b, 2)
    dout = project(lax.axis_index("tp"), out_weight, [grad_out, *pieces[::-1]])
    kx_three = hop(pick(k_three, 3), 1)
    far_keys = (k_one, k_two, k_three, stack(x_own[:BLK], kx_near[:BLK]), kx_near[BLK:], kx_three)
    dv, probs, dv_one, dv_two, dv_three, dvx_own, dvx_one, dvx_two, dvx_three = in_vmem(
        value_kernel, scalars, (queries, dout, keys, *far_keys),
        [(row_count, f32), ((row_count,), bf16)] + far_outs + [(BLK, bf16)] * 4, 2, feature_width,
    )
    dvx_three = hop(dvx_three, 1)
    v_two, v_one, dvx_two, dvx_three, dvx_one = tied(v_two, v_one, dvx_two, dvx_three, dvx_one)
    dv_three = sum_three(dv_three, dvx_three)
    swapped = hop(jnp.where(at_end, dv_three, v_two), 2)
    vx_near = hop(stack(pick(v_one, 1), pick(v_two, 2)), 1)
    dvx_one, dv_three = tied(hop(dvx_one, 1), dv_three)
    own_across = across(dv_three)
    swapped, dv_one = tied(swapped, sum_one(dv_one, dvx_one))
    v_three = jnp.where(at_end, swapped, v_across)
    in_three = jnp.where(at_end, 0, swapped)
    vx_three = hop(pick(v_three, 3), 1)
    dv_one = hop(dv_one, 2)
    vx_three, vx_near, dvx_two, own_across = tied(vx_three, vx_near, dvx_two, own_across)
    dvx_two = hop(dvx_two, 1)
    ds, dk_one, dk_two, dk_three, dkx_own, dkx_near, dkx_three = in_vmem(
        functools.partial(key_kernel, 0), scalars,
        (queries, dout, probs, values, v_one, v_two, v_three,
         stack(x_own[BLK:], vx_near[:BLK]), vx_near[BLK:], vx_three),
        [((row_count,), bf16)] + far_outs + [(BLK, bf16), (2 * BLK, bf16), (BLK, bf16)],
        2, feature_width,
    )
    dkx_three, dkx_near, dvx_two = tied(dkx_three, dkx_near, dvx_two)
    dkx_three = hop(dkx_three, 1)
    dv_two = hop(sum_two(dv_two, dvx_two, in_three), 4)
    dkx_three, dkx_near, dv_one = tied(dkx_three, dkx_near, dv_one)
    dk_three = hop(sum_three(dk_three, dkx_three), 2)
    dkx_near = hop(dkx_near, 1)
    dq, dk = in_vmem(
        query_kernel, scalars, (queries, ds, keys, *far_keys),
        [(row_count, bf16), (row_count, f32)], 1, feature_width,
    )
    dk_three, dkx_near, dq, dv_two = tied(dk_three, dkx_near, dq, dv_two)
    dk_two = hop(sum_two(dk_two, dkx_near[BLK:], dk_three), 4)
    dk_one = hop(sum_one(dk_one, dkx_near[:BLK]), 2)
    x_own = hop(stack(dvx_own, dkx_own), 1)
    grad_values = total(dv + jnp.where(at_end, 0, own_across).astype(f32), x_own[:BLK], dv_one, dv_two)
    grad_keys = total(dk, x_own[BLK:], dk_one, dk_two)
    return (dq, grad_keys, grad_values)


def solution(mesh):
    placed = (
        P("seq", "tp"),
        P("tp", None),
        P("seq", "tp"),
        P("seq", "tp"),
        P("seq", "tp"),
        P(),
        P(),
    )
    return jax.shard_map(
        shards_cube if mesh.shape["seq"] == CUBE else shards_general,
        mesh=mesh,
        in_specs=placed,
        out_specs=(P("seq", "tp"), P("seq", "tp"), P("seq", "tp")),
        check_vma=False,
    )
```

```python
import functools
import math

import jax
import jax.numpy as jnp
from jax import lax
from jax.experimental import pallas as pl
from jax.experimental.pallas import tpu as pltpu
from jax.sharding import PartitionSpec as P

D_HEAD = 128
BLK = 128
BLK_DEV = 2
NREM = 3


def project_part(out_weight, piece):
    return lax.dot_general(
        piece, out_weight, (((1,), (1,)), ((), ())), preferred_element_type=jnp.float32
    )


def attend_group(query_group, dout_group, key_far, value_far, seen_mask, key_near, value_near):
    scaling = 1.0 / math.sqrt(D_HEAD)
    near_scores = (
        jnp.einsum("aihd,jhd->ahij", query_group, key_near, preferred_element_type=jnp.float32)
        * scaling
    )
    far_scores = (
        jnp.einsum("aihd,ajhd->ahij", query_group, key_far, preferred_element_type=jnp.float32)
        * scaling
    )
    far_scores = jnp.where(seen_mask[:, None, None, :], far_scores, -1e30)
    highest = jnp.maximum(jnp.max(near_scores, axis=3), jnp.max(far_scores, axis=3))[..., None]
    near_exp = jnp.exp(near_scores - highest)
    far_exp = jnp.exp(far_scores - highest)
    totals = jnp.sum(near_exp, axis=3, keepdims=True) + jnp.sum(far_exp, axis=3, keepdims=True)
    near_probs = near_exp / totals
    far_probs = far_exp / totals
    near_grad = jnp.einsum(
        "aihd,jhd->ahij", dout_group, value_near, preferred_element_type=jnp.float32
    )
    far_grad = jnp.einsum(
        "aihd,ajhd->ahij", dout_group, value_far, preferred_element_type=jnp.float32
    )
    row_delta = jnp.sum(near_probs * near_grad, axis=3, keepdims=True) + jnp.sum(
        far_probs * far_grad, axis=3, keepdims=True
    )
    near_ds = (near_probs * (near_grad - row_delta) * scaling).astype(jnp.bfloat16)
    far_ds = (far_probs * (far_grad - row_delta) * scaling).astype(jnp.bfloat16)
    grad_query = jnp.einsum("ahij,jhd->aihd", near_ds, key_near, preferred_element_type=jnp.float32)
    grad_query = grad_query + jnp.einsum(
        "ahij,ajhd->aihd", far_ds, key_far, preferred_element_type=jnp.float32
    )
    log_totals = (highest + jnp.log(totals))[..., 0]
    return (
        near_probs,
        far_probs,
        near_ds,
        far_ds,
        grad_query.astype(jnp.bfloat16),
        log_totals,
        row_delta[..., 0],
    )


def shards_general(grad_out, out_weight, queries, keys, values, visible, live):
    shard_count = lax.axis_size("seq")
    myself = lax.axis_index("seq")
    row_count, feature_width = queries.shape
    head_count = feature_width // D_HEAD
    entries = BLK_DEV * NREM
    capacity = min(BLK_DEV, -(-entries // (shard_count - 1)))
    slot_count = shard_count * capacity
    dout = project_part(out_weight, lax.all_gather(grad_out, "tp", axis=1, tiled=True)).astype(
        jnp.bfloat16
    )
    owners = (visible // BLK_DEV).reshape(shard_count, entries)
    block_within = (visible % BLK_DEV).reshape(shard_count, entries)
    living = (jnp.arange(NREM, dtype=jnp.int32)[None, :] < live[:, None]).reshape(
        shard_count, entries
    )
    positions = jnp.arange(entries, dtype=jnp.int32)
    earlier = positions[None, :] < positions[:, None]
    matching = (owners[:, :, None] == owners[:, None, :]) & living[:, None, :] & earlier[None, :, :]
    ranking = jnp.sum(matching.astype(jnp.int32), axis=2)
    slot_ids = jnp.arange(capacity, dtype=jnp.int32)
    chosen = (living & (owners == myself))[:, None, :] & (
        ranking[:, None, :] == slot_ids[None, :, None]
    )
    filled = jnp.any(chosen, axis=2).reshape(slot_count)
    send_index = jnp.sum(jnp.where(chosen, block_within[:, None, :], 0), axis=2).reshape(slot_count)
    key_blocks = keys.reshape(BLK_DEV, BLK, feature_width)
    value_blocks = values.reshape(BLK_DEV, BLK, feature_width)
    keep_slot = filled[:, None, None]
    send_keys = jnp.where(
        keep_slot, jnp.take(key_blocks, send_index, axis=0), jnp.zeros((), keys.dtype)
    )
    send_values = jnp.where(
        keep_slot, jnp.take(value_blocks, send_index, axis=0), jnp.zeros((), values.dtype)
    )
    fetched_keys, fetched_values = (
        lax.all_to_all(
            send_keys.reshape(shard_count, capacity, BLK, feature_width),
            "seq",
            split_axis=0,
            concat_axis=0,
            tiled=True,
        ),
        lax.all_to_all(
            send_values.reshape(shard_count, capacity, BLK, feature_width),
            "seq",
            split_axis=0,
            concat_axis=0,
            tiled=True,
        ),
    )
    my_owners = lax.dynamic_index_in_dim(owners, myself, 0, keepdims=False)
    my_ranks = lax.dynamic_index_in_dim(ranking, myself, 0, keepdims=False)
    my_living = lax.dynamic_index_in_dim(living, myself, 0, keepdims=False)
    fetch_index = my_owners * capacity + my_ranks
    key_far = jnp.take(fetched_keys.reshape(slot_count, BLK, feature_width), fetch_index, axis=0)
    value_far = jnp.take(
        fetched_values.reshape(slot_count, BLK, feature_width), fetch_index, axis=0
    )
    placement = (
        (jnp.arange(slot_count, dtype=jnp.int32)[:, None] == fetch_index[None, :])
        & my_living[None, :]
    ).astype(jnp.bfloat16)
    collect = (
        (jnp.arange(BLK_DEV, dtype=jnp.int32)[:, None] == send_index[None, :]) & filled[None, :]
    ).astype(jnp.bfloat16)
    group_size = math.gcd(BLK_DEV, max(1, 512 // BLK))
    group_count = BLK_DEV // group_size

    def grouped(array_in):
        return array_in.reshape((group_count, group_size) + array_in.shape[1:])

    query_blocks = grouped(queries.reshape(BLK_DEV, BLK, head_count, D_HEAD))
    dout_blocks = grouped(dout.reshape(BLK_DEV, BLK, head_count, D_HEAD))
    far_key_blocks = grouped(key_far.reshape(BLK_DEV, NREM * BLK, head_count, D_HEAD))
    far_value_blocks = grouped(value_far.reshape(BLK_DEV, NREM * BLK, head_count, D_HEAD))
    seen_blocks = grouped(jnp.repeat(my_living.reshape(BLK_DEV, NREM), BLK, axis=1))
    key_near = keys.reshape(row_count, head_count, D_HEAD)
    value_near = values.reshape(row_count, head_count, D_HEAD)

    def one_group(carry, inputs):
        near_key_acc, near_value_acc = carry
        query_group, dout_group, key_group, value_group, mask_group = inputs
        near_probs, far_probs, near_ds, far_ds, grad_query, log_totals, row_delta = attend_group(
            query_group, dout_group, key_group, value_group, mask_group, key_near, value_near
        )
        near_key_acc = near_key_acc + jnp.einsum(
            "ahij,aihd->jhd", near_ds, query_group, preferred_element_type=jnp.float32
        )
        near_value_acc = near_value_acc + jnp.einsum(
            "ahij,aihd->jhd",
            near_probs.astype(jnp.bfloat16),
            dout_group,
            preferred_element_type=jnp.float32,
        )
        far_key_term = jnp.einsum(
            "ahij,aihd->ajhd", far_ds, query_group, preferred_element_type=jnp.float32
        ).astype(jnp.bfloat16)
        far_value_term = jnp.einsum(
            "ahij,aihd->ajhd",
            far_probs.astype(jnp.bfloat16),
            dout_group,
            preferred_element_type=jnp.float32,
        ).astype(jnp.bfloat16)
        extra = (far_key_term, far_value_term)
        return ((near_key_acc, near_value_acc), (grad_query, extra))

    start = (
        jnp.zeros((row_count, head_count, D_HEAD), jnp.float32),
        jnp.zeros((row_count, head_count, D_HEAD), jnp.float32),
    )
    (near_keys, near_values), (grad_query_all, extra_all) = lax.scan(
        one_group, start, (query_blocks, dout_blocks, far_key_blocks, far_value_blocks, seen_blocks)
    )
    grad_queries = grad_query_all.reshape(row_count, feature_width)
    far_key_terms = extra_all[0].reshape(entries, BLK * feature_width)
    far_value_terms = extra_all[1].reshape(entries, BLK * feature_width)
    returned_keys = jnp.dot(placement, far_key_terms, preferred_element_type=jnp.float32).astype(
        jnp.bfloat16
    )
    returned_values = jnp.dot(
        placement, far_value_terms, preferred_element_type=jnp.float32
    ).astype(jnp.bfloat16)
    back_keys, back_values = (
        lax.all_to_all(
            returned_keys.reshape(shard_count, capacity, BLK, feature_width),
            "seq",
            split_axis=0,
            concat_axis=0,
            tiled=True,
        ),
        lax.all_to_all(
            returned_values.reshape(shard_count, capacity, BLK, feature_width),
            "seq",
            split_axis=0,
            concat_axis=0,
            tiled=True,
        ),
    )
    far_key_sum = jnp.dot(
        collect,
        back_keys.reshape(slot_count, BLK * feature_width),
        preferred_element_type=jnp.float32,
    )
    far_value_sum = jnp.dot(
        collect,
        back_values.reshape(slot_count, BLK * feature_width),
        preferred_element_type=jnp.float32,
    )
    grad_keys = (
        near_keys.reshape(row_count, feature_width) + far_key_sum.reshape(row_count, feature_width)
    ).astype(jnp.bfloat16)
    grad_values = (
        near_values.reshape(row_count, feature_width)
        + far_value_sum.reshape(row_count, feature_width)
    ).astype(jnp.bfloat16)
    return (grad_queries, grad_keys, grad_values)


CUBE = 8
SLOTS = 10
VMEM_LIMIT = 14 * 1024 * 1024
SEEN = (BLK_DEV + NREM) * BLK
SMALL = pl.CostEstimate(flops=1, bytes_accessed=1, transcendentals=0)
SCALING = 1.0 / math.sqrt(D_HEAD)


def slot_of(me, visible_ref, a, j):
    listed = visible_ref[(me * BLK_DEV + a) * NREM + j]
    apart = (listed // BLK_DEV) ^ me
    row = apart // 2
    return jnp.where(apart % 2 == 0, (row - 1) * BLK_DEV + listed % BLK_DEV, 6 + row)


def entries_of(me_ref, visible_ref, live_ref):
    me = me_ref[0]
    slots = [[slot_of(me, visible_ref, a, j) for j in range(NREM)] for a in range(BLK_DEV)]
    return slots, [live_ref[me * BLK_DEV + a] for a in range(BLK_DEV)]


def dot(a, b):
    return jnp.dot(a, b, preferred_element_type=jnp.float32)


def dot_nt(a, b):
    return lax.dot_general(a, b, (((1,), (1,)), ((), ())), preferred_element_type=jnp.float32)


def dot_tn(a, b):
    return lax.dot_general(a, b, (((0,), (0,)), ((), ())), preferred_element_type=jnp.float32)


def blocks_of(refs):
    return [(ref, i * BLK) for ref in refs for i in range(ref.shape[0] // BLK)]


def fill(refs, slots_ref):
    def one_head(head, columns):
        for at, (ref, row) in enumerate(blocks_of(refs)):
            slots_ref[at, :, columns] = ref[row : row + BLK, columns]

    over_heads(slots_ref.shape[2] // D_HEAD, 1, one_head)


def clear(slots_ref):
    def one_head(head, columns):
        for at in range(slots_ref.shape[0]):
            slots_ref[at, :, columns] = jnp.zeros((BLK, D_HEAD), slots_ref.dtype)

    over_heads(slots_ref.shape[2] // D_HEAD, 1, one_head)


def drain(slots_ref, refs):
    def one_head(head, columns):
        for at, (ref, row) in enumerate(blocks_of(refs)):
            ref[row : row + BLK, columns] = slots_ref[at, :, columns]

    over_heads(slots_ref.shape[2] // D_HEAD, 1, one_head)


def softmax_t(near, far, live):
    near = near * SCALING
    far = jnp.concatenate(
        [
            jnp.where(j < live, far[j * BLK : (j + 1) * BLK] * SCALING, -1e30)
            for j in range(NREM)
        ],
        axis=0,
    )
    highest = jnp.maximum(
        jnp.max(near, axis=0, keepdims=True), jnp.max(far, axis=0, keepdims=True)
    )
    near = jnp.exp(near - highest)
    far = jnp.exp(far - highest)
    total = jnp.sum(near, axis=0, keepdims=True) + jnp.sum(far, axis=0, keepdims=True)
    return near / total, far / total


def over_heads(head_count, unroll, body):
    @pl.loop(0, head_count // unroll)
    def _(i):
        for u in range(unroll):
            head = i * unroll + u
            body(head, pl.ds(pl.multiple_of(head * D_HEAD, D_HEAD), D_HEAD))


def value_kernel(me_ref, visible_ref, live_ref, q, do, k, *refs):
    key_refs, (dv, probs), out_refs, (k_slots, out_slots) = refs[:6], refs[6:8], refs[8:-2], refs[-2:]
    slots, lives = entries_of(me_ref, visible_ref, live_ref)
    clear(out_slots)
    fill(key_refs, k_slots)

    def one_head(head, columns):
        near_scores = dot_nt(k[:, columns], q[:, columns])
        near_probs = []
        for a in range(BLK_DEV):
            rows = slice(a * BLK, (a + 1) * BLK)
            far_k = jnp.concatenate([k_slots[s, :, columns] for s in slots[a]], axis=0)
            near_p, far_p = softmax_t(
                near_scores[:, rows], dot_nt(far_k, q[rows, columns]), lives[a]
            )
            near_probs.append(near_p.astype(jnp.bfloat16))
            far_p = far_p.astype(jnp.bfloat16)
            probs[head, BLK_DEV * BLK :, rows] = far_p
            far_term = dot(far_p, do[rows, columns]).astype(jnp.bfloat16)
            for j, s in enumerate(slots[a]):
                out_slots[s, :, columns] = far_term[j * BLK : (j + 1) * BLK]
        near_probs = jnp.concatenate(near_probs, axis=1)
        probs[head, : BLK_DEV * BLK, :] = near_probs
        dv[:, columns] = dot(near_probs, do[:, columns])

    over_heads(q.shape[1] // D_HEAD, 8, one_head)
    drain(out_slots, out_refs)


def key_kernel(first, me_ref, visible_ref, live_ref, q, do, probs, v, one, two, three, near, x_two, x_three, *refs):
    ds, out_refs, (v_slots, out_slots) = refs[0], refs[1:-2], refs[-2:]
    slots, _ = entries_of(me_ref, visible_ref, live_ref)
    clear(out_slots)
    fill((one, two, three, near, x_two, x_three), v_slots)

    def one_head(head, columns):
        whole = pl.ds(pl.multiple_of((first + head) * D_HEAD, D_HEAD), D_HEAD)
        near_grads = dot_nt(v[:, whole], do[:, whole])
        for a in range(BLK_DEV):
            rows = slice(a * BLK, (a + 1) * BLK)
            far_v = jnp.concatenate([v_slots[s, :, columns] for s in slots[a]], axis=0)
            near_g, far_g = near_grads[:, rows], dot_nt(far_v, do[rows, whole])
            near_p = probs[first + head, : BLK_DEV * BLK, rows].astype(jnp.float32)
            far_p = probs[first + head, BLK_DEV * BLK :, rows].astype(jnp.float32)
            delta = jnp.sum(near_p * near_g, axis=0, keepdims=True) + jnp.sum(
                far_p * far_g, axis=0, keepdims=True
            )
            ds[head, : BLK_DEV * BLK, rows] = (near_p * (near_g - delta) * SCALING).astype(
                jnp.bfloat16
            )
            far_ds = (far_p * (far_g - delta) * SCALING).astype(jnp.bfloat16)
            ds[head, BLK_DEV * BLK :, rows] = far_ds
            far_term = dot(far_ds, q[rows, whole]).astype(jnp.bfloat16)
            for j, s in enumerate(slots[a]):
                out_slots[s, :, columns] = far_term[j * BLK : (j + 1) * BLK]

    over_heads(ds.shape[0], 8, one_head)
    drain(out_slots, out_refs)


def query_kernel(me_ref, visible_ref, live_ref, q, ds, k, *refs):
    key_refs, dq, dk, k_slots = refs[:6], refs[6], refs[7], refs[8]
    slots, _ = entries_of(me_ref, visible_ref, live_ref)
    fill(key_refs, k_slots)

    def one_head(head, columns):
        near_ds = ds[head, : BLK_DEV * BLK, :]
        near_dq = dot_tn(near_ds, k[:, columns])
        dk[:, columns] = dot(near_ds, q[:, columns])
        for a in range(BLK_DEV):
            rows = slice(a * BLK, (a + 1) * BLK)
            far_k = jnp.concatenate([k_slots[s, :, columns] for s in slots[a]], axis=0)
            far_dq = dot_tn(ds[head, BLK_DEV * BLK :, rows], far_k)
            dq[rows, columns] = (near_dq[rows] + far_dq).astype(jnp.bfloat16)

    over_heads(q.shape[1] // D_HEAD, 8, one_head)


def in_vmem(kernel, scalars, arrays, outs, scratch_count, width):
    vmem = pl.BlockSpec(memory_space=pltpu.VMEM)
    return pl.pallas_call(
        kernel,
        out_shape=[
            jax.ShapeDtypeStruct(
                (width // D_HEAD, SEEN, rows[0]) if isinstance(rows, tuple) else (rows, width), kind
            )
            for rows, kind in outs
        ],
        in_specs=[pl.BlockSpec(memory_space=pltpu.SMEM)] * len(scalars) + [vmem] * len(arrays),
        out_specs=[vmem] * len(outs),
        scratch_shapes=[pltpu.VMEM((SLOTS, BLK, width), jnp.bfloat16)] * scratch_count,
        compiler_params=pltpu.CompilerParams(vmem_limit_bytes=VMEM_LIMIT),
        cost_estimate=SMALL,
    )(*scalars, *arrays)


def dout_kernel(me_ref, weight, *refs):
    pieces, dout = refs[:-1], refs[-1]
    width = pieces[0].shape[1]
    total = None
    for d, piece in enumerate(pieces):
        columns = pl.ds(pl.multiple_of((me_ref[0] ^ d) * width, width), width)
        part = dot_nt(piece[...], weight[:, columns])
        total = part if total is None else total + part
    dout[...] = total.astype(jnp.bfloat16)


def project(tp_index, out_weight, pieces):
    rows, width = pieces[0].shape
    features = out_weight.shape[0]
    tile = min(256, features)
    return pl.pallas_call(
        dout_kernel,
        out_shape=jax.ShapeDtypeStruct((rows, features), jnp.bfloat16),
        grid_spec=pltpu.PrefetchScalarGridSpec(
            num_scalar_prefetch=1,
            grid=(features // tile,),
            in_specs=[pl.BlockSpec((tile, out_weight.shape[1]), lambda i, *_: (i, 0))]
            + [pl.BlockSpec((rows, width), lambda i, *_: (0, 0))] * len(pieces),
            out_specs=pl.BlockSpec((rows, tile), lambda i, *_: (0, i)),
        ),
        compiler_params=pltpu.CompilerParams(vmem_limit_bytes=VMEM_LIMIT),
        cost_estimate=SMALL,
    )(tp_index.reshape(1), out_weight, *pieces)


def tied(*arrays):
    return lax.optimization_barrier(arrays)


def shards_cube(grad_out, out_weight, queries, keys, values, visible, live):
    myself = lax.axis_index("seq")
    row_count, feature_width = queries.shape
    other = myself ^ 1
    f32, bf16 = jnp.float32, jnp.bfloat16

    def hop(array, distance, axis="seq"):
        size = lax.axis_size(axis)
        return lax.ppermute(array, axis, [(i, i ^ distance) for i in range(size)])

    listed = lax.dynamic_slice_in_dim(visible, other * BLK_DEV, BLK_DEV, 0).reshape(-1)
    apart = (listed // BLK_DEV) ^ other
    wanted = [jnp.sum(jnp.where(apart == 2 * r + 1, listed % BLK_DEV, 0)) for r in range(CUBE // 2)]

    def pick(array, r):
        return lax.dynamic_slice_in_dim(array, wanted[r] * BLK, BLK, 0)

    def place(block, r):
        row = lax.broadcasted_iota(jnp.int32, (row_count, 1), 0) // BLK
        return jnp.where(row == wanted[r], jnp.concatenate([block, block], axis=0), 0).astype(f32)

    scalars = (myself.reshape(1), visible.reshape(-1), live)
    far_outs = [(2 * BLK, bf16)] * 3

    def stack(*blocks):
        return jnp.concatenate(blocks, axis=0)

    def sum_one(one, x_one):
        return (one.astype(f32) + place(x_one, 1)).astype(bf16)

    def sum_three(three, far):
        return (three.astype(f32) + place(far, 3)).astype(bf16)

    def sum_two(two, x_two, three):
        return (two.astype(f32) + place(x_two, 2) + three.astype(f32)).astype(bf16)

    def total(near, x_own, one, two):
        return (near + place(x_own, 0) + one.astype(f32) + two.astype(f32)).astype(bf16)

    at_end = (myself // 2 == 0) | (myself // 2 == 3)

    def across(array):
        ends = [(i, i) for i in (0, 1, 6, 7)]
        return lax.ppermute(array, "seq", ends + [(2, 4), (3, 5), (4, 2), (5, 3)])

    k_two = hop(keys, 4)
    k_one = hop(keys, 2)
    pieces = [hop(grad_out, d, "tp") for d in range(lax.axis_size("tp") - 1, 0, -1)]
    pieces[-1], keys_b, values_b, at_end = tied(pieces[-1], keys, values, at_end)
    x_own = hop(stack(pick(keys_b, 0), pick(values_b, 0)), 1)
    k_one, k_two, values_b, x_own = tied(k_one, k_two, values_b, x_own)
    k_three = hop(k_two, 2)
    v_across = across(values_b)
    kx_near = hop(stack(pick(k_one, 1), pick(k_two, 2)), 1)
    k_three, values_b, v_across, *pieces = tied(k_three, values_b, v_across, *pieces)
    v_two = hop(values_b, 4)
    v_one = hop(values_b, 2)
    dout = project(lax.axis_index("tp"), out_weight, [grad_out, *pieces[::-1]])
    kx_three = hop(pick(k_three, 3), 1)
    far_keys = (k_one, k_two, k_three, stack(x_own[:BLK], kx_near[:BLK]), kx_near[BLK:], kx_three)
    dv, probs, dv_one, dv_two, dv_three, dvx_own, dvx_one, dvx_two, dvx_three = in_vmem(
        value_kernel, scalars, (queries, dout, keys, *far_keys),
        [(row_count, f32), ((row_count,), bf16)] + far_outs + [(BLK, bf16)] * 4, 2, feature_width,
    )
    dvx_three = hop(dvx_three, 1)
    v_two, v_one, dvx_two, dvx_three, dvx_one = tied(v_two, v_one, dvx_two, dvx_three, dvx_one)
    dv_three = sum_three(dv_three, dvx_three)
    swapped = hop(jnp.where(at_end, dv_three, v_two), 2)
    vx_near = hop(stack(pick(v_one, 1), pick(v_two, 2)), 1)
    dvx_one, dv_three = tied(hop(dvx_one, 1), dv_three)
    own_across = across(dv_three)
    swapped, dv_one = tied(swapped, sum_one(dv_one, dvx_one))
    v_three = jnp.where(at_end, swapped, v_across)
    in_three = jnp.where(at_end, 0, swapped)
    vx_three = hop(pick(v_three, 3), 1)
    dv_one = hop(dv_one, 2)
    vx_three, vx_near, dvx_two, own_across = tied(vx_three, vx_near, dvx_two, own_across)
    dvx_two = hop(dvx_two, 1)
    ds, dk_one, dk_two, dk_three, dkx_own, dkx_near, dkx_three = in_vmem(
        functools.partial(key_kernel, 0), scalars,
        (queries, dout, probs, values, v_one, v_two, v_three,
         stack(x_own[BLK:], vx_near[:BLK]), vx_near[BLK:], vx_three),
        [((row_count,), bf16)] + far_outs + [(BLK, bf16), (2 * BLK, bf16), (BLK, bf16)],
        2, feature_width,
    )
    dkx_three, dkx_near, dvx_two = tied(dkx_three, dkx_near, dvx_two)
    dkx_three = hop(dkx_three, 1)
    dv_two = hop(sum_two(dv_two, dvx_two, in_three), 4)
    dkx_three, dkx_near, dv_one = tied(dkx_three, dkx_near, dv_one)
    dk_three = hop(sum_three(dk_three, dkx_three), 2)
    dkx_near = hop(dkx_near, 1)
    dq, dk = in_vmem(
        query_kernel, scalars, (queries, ds, keys, *far_keys),
        [(row_count, bf16), (row_count, f32)], 1, feature_width,
    )
    dk_three, dkx_near, dq, dv_two = tied(dk_three, dkx_near, dq, dv_two)
    dk_two = hop(sum_two(dk_two, dkx_near[BLK:], dk_three), 4)
    dk_one = hop(sum_one(dk_one, dkx_near[:BLK]), 2)
    x_own = hop(stack(dvx_own, dkx_own), 1)
    grad_values = total(dv + jnp.where(at_end, 0, own_across).astype(f32), x_own[:BLK], dv_one, dv_two)
    grad_keys = total(dk, x_own[BLK:], dk_one, dk_two)
    return (dq, grad_keys, grad_values)


def solution(mesh):
    placed = (
        P("seq", "tp"),
        P("tp", None),
        P("seq", "tp"),
        P("seq", "tp"),
        P("seq", "tp"),
        P(),
        P(),
    )
    return jax.shard_map(
        shards_cube if mesh.shape["seq"] == CUBE else shards_general,
        mesh=mesh,
        in_specs=placed,
        out_specs=(P("seq", "tp"), P("seq", "tp"), P("seq", "tp")),
        check_vma=False,
    )
```
